32 devices in a mesh: ctx: 4 (over y, core), fsdp: 8 (over z, x).
Axes of the slice: x: 2, y: 2, z: 4, core: 2. Of those that a mesh axis runs over, the one named last changes fastest.
Arguments:
- hidden: bfloat16 [4, 8, 256, 2048], P('ctx', 'fsdp'), may hold values from -4.5 to 4.5
- norm_gain: float32 [2048], replicated, may hold values from 0.1 to 1.9
- w_query: bfloat16 [2048, 2048], P('fsdp', 'ctx'), may hold values from -1 to 1
- w_key: bfloat16 [2048, 1024], P('fsdp', 'ctx'), may hold values from -1 to 1
- w_value: bfloat16 [2048, 1024], P('fsdp', 'ctx'), may hold values from -0.125 to 0.125
- q_gain: float32 [128], replicated, may hold values from 0.5 to 5
- k_gain: float32 [128], replicated, may hold values from 0.5 to 5
- lengths: int32 [8, 4], replicated, may hold values from 1 to 512, 1024 in all within a row
- piece_map: int32 [8, 4], replicated, may hold values from 0 to 3, each once within a row
- owner: int32 [4, 8, 256], P('ctx', 'fsdp'), may hold values from 0 to 31, as said below
- slot: int32 [4, 8, 256], P('ctx', 'fsdp'), may hold values from 0 to 511, as said below
Outputs:
- attended: bfloat16 [4, 8, 256, 2048], P('ctx', 'fsdp')
- cache: bfloat16 [16384, 2048], P(('ctx', 'fsdp'))
The draws below stay inside these ranges and needn't reach their ends.
Inputs may be any that keep to these rules, and one draw needn't show every extreme that they name: `lengths`: each row sums to 1024; its largest entry is 512. `piece_map`: each row holds every piece once. At most 16 tokens of one device go to one owner; in every draw one owner receives exactly 16 from every device. `slot`: tokens with the same owner have distinct slots.
All inputs are finite; a program needn't handle non-finite values.
Results may differ from the reference program's by a relative error of at most 0.0035.
The reference program's roundings to bfloat16 on the way count: a program that leaves them out, or rounds other values in their place, can miss the bound.
Values may be sent and summed in bfloat16 or wider, within the bound.
A program may use at most 128 MiB of HBM per device.

```python
import math
import jax
import jax.numpy as jnp
import numpy as np
from jax import lax

MODEL_WIDTH = 2048
QUERY_HEADS = 16
KEY_VALUE_HEADS = 8
HEAD_WIDTH = 128
TOK_DEV = 256
NSEG = 4
QW = 2048
KW = 1024
PIECES = 4
GROUPS = 8
STREAM_TOKENS = 1024
LONGEST = 512
OWNERS = 32
MOST = 16
CAP = 512


def route_tables(key):
    base_key = jax.random.fold_in(key, 11)
    heavy_key, source_key, table_key = jax.random.split(base_key, 3)
    heavy_owner = jax.random.randint(heavy_key, (), 0, OWNERS)

    def one_source(sub_key):
        first_key, second_key, third_key = jax.random.split(sub_key, 3)
        spread = jax.random.permutation(first_key, (OWNERS - 1) * MOST)[:TOK_DEV - MOST]
        other_owner = (heavy_owner + 1 + spread // MOST) % OWNERS
        other_rank = spread % MOST
        heavy_rank = jax.random.permutation(second_key, MOST)
        owner_list = jnp.concatenate([jnp.full((MOST,), heavy_owner, jnp.int32), other_owner.astype(jnp.int32)])
        rank_list = jnp.concatenate([heavy_rank.astype(jnp.int32), other_rank.astype(jnp.int32)])
        shuffle = jax.random.permutation(third_key, TOK_DEV)
        return (owner_list[shuffle], rank_list[shuffle])
    owners, rank_list = jax.vmap(one_source)(jax.random.split(source_key, OWNERS))
    tables = jax.vmap(lambda sub_key: jax.random.permutation(sub_key, CAP).astype(jnp.int32))(jax.random.split(table_key, OWNERS))
    sources = jnp.arange(OWNERS, dtype=jnp.int32)[:, None]
    slot_ids = tables[owners, sources * MOST + rank_list]
    return (owners.reshape(PIECES, GROUPS, TOK_DEV), slot_ids.astype(jnp.int32).reshape(PIECES, GROUPS, TOK_DEV))


def draw_owner(key, part):
    return route_tables(key)[0]


def draw_slot(key, part):
    return route_tables(key)[1]


def projection_tables(key):
    base_key = jax.random.fold_in(key, 17)
    query_key, jitter_seed = jax.random.split(base_key, 2)
    query_matrix = jnp.clip(0.4 * jax.random.normal(query_key, (MODEL_WIDTH, QW), jnp.float32), -1.0, 1.0)
    key_table = jnp.clip(0.4 * jax.random.normal(jitter_seed, (MODEL_WIDTH, KW), jnp.float32), -1.0, 1.0)
    return (query_matrix, key_table)


def draw_w_query(key, part):
    return projection_tables(key)[0].astype(jnp.bfloat16)


def draw_w_key(key, part):
    return projection_tables(key)[1].astype(jnp.bfloat16)


def draw_hidden(key, part):
    sub_key = jax.random.fold_in(key, 7)
    first_key = jax.random.fold_in(sub_key, 0)
    full_shape = (PIECES, GROUPS, TOK_DEV, MODEL_WIDTH)
    values = jnp.clip(jax.random.normal(first_key, full_shape, jnp.float32), -4.5, 4.5)
    return values.astype(jnp.bfloat16)


def draw_q_gain(key, part):
    sub_key = jax.random.fold_in(key, 3)
    return jax.random.uniform(sub_key, (HEAD_WIDTH,), jnp.float32, 0.5, 2.0)


def draw_k_gain(key, part):
    sub_key = jax.random.fold_in(key, 5)
    return jax.random.uniform(sub_key, (HEAD_WIDTH,), jnp.float32, 0.5, 2.0)


def block_scale(stream_key, dims, cuts, least, top_value):
    level, own = 1.0, jax.random.fold_in(stream_key, 6)
    for dim, parts in cuts:
        draws = jnp.exp(jax.random.uniform(jax.random.fold_in(own, dim), (parts,), jnp.float32, least / len(cuts), top_value / len(cuts)))
        level = level * jnp.repeat(draws, dims[dim] // parts).reshape([-1 if axis == dim else 1 for axis in range(len(dims))])
    return level


def profile(count, total, most, skew):
    portions = [(1 << 20) // math.isqrt(grade ** skew) + 1 for grade in range(2, count + 1)]
    spare, given = total - most - (count - 1), [1] * (count - 1)
    while spare > 0:
        candidates = [i for i in range(count - 1) if given[i] < most]
        mass, left = sum([portions[i] for i in candidates]), spare
        for i in candidates:
            more = min(most - given[i], max(1, left * portions[i] // mass), spare)
            given[i] = given[i] + more
            spare = spare - more
    return np.array([most] + given)


def uneven_parts(own_key, number_of, total, bound, slope):
    if number_of == 2:
        one = jax.random.randint(own_key, (), max(1, total - bound), min(bound, total - 1) + 1)
        return jnp.stack([one, total - one])
    sizes = jnp.asarray(profile(number_of, total, bound, slope), jnp.int32)
    pairs = (number_of - 1) // 2
    source_of, taker = sizes[1:1 + 2 * pairs:2], sizes[2:2 + 2 * pairs:2]
    room = jnp.minimum(source_of - 1, bound - taker)
    shifted = jax.random.randint(jax.random.fold_in(own_key, 1), (pairs,), 0, 1 << 20) % (room + 1)
    sizes = sizes.at[1:1 + 2 * pairs:2].set(source_of - shifted).at[2:2 + 2 * pairs:2].set(taker + shifted)
    return sizes[jax.random.permutation(jax.random.fold_in(own_key, 2), number_of)]


def bell_draw(rng, shape, scale, most, cuts=(), kind=jnp.bfloat16):
    drawn = scale * jax.random.normal(rng, shape, jnp.float32)
    if cuts:
        drawn = drawn * block_scale(rng, shape, cuts, -0.22, 0.18)
    return jnp.clip(drawn, -most, most).astype(kind)


def setup_inputs(seed: int = 0) -> dict:
    splits = jax.random.split(jax.random.key(seed), 12)
    hidden = draw_hidden(jax.random.fold_in(splits[11], 71), 0)
    norm_gain = jnp.clip(1.0 + 0.18 * jax.random.normal(splits[1], (MODEL_WIDTH,), jnp.float32), 0.1, 1.9)
    w_query = draw_w_query(jax.random.fold_in(splits[11], 71), 0)
    w_key = draw_w_key(jax.random.fold_in(splits[11], 71), 0)
    w_value = bell_draw(splits[4], (MODEL_WIDTH, KW), MODEL_WIDTH ** -0.5, 0.125, ((0, 8), (1, 4)))
    q_gain = draw_q_gain(jax.random.fold_in(splits[11], 71), 0)
    k_gain = draw_k_gain(jax.random.fold_in(splits[11], 71), 0)
    lengths = jax.vmap(lambda own: uneven_parts(own, NSEG, STREAM_TOKENS, LONGEST, 2))(jax.random.split(splits[7], GROUPS)).reshape((GROUPS, NSEG)).astype(jnp.int32)
    piece_map = jax.vmap(lambda own: jax.random.permutation(own, PIECES))(jax.random.split(splits[8], GROUPS)).reshape((GROUPS, PIECES)).astype(jnp.int32)
    owner = draw_owner(jax.random.fold_in(splits[11], 71), 0)
    slot = draw_slot(jax.random.fold_in(splits[11], 71), 0)
    return {"hidden": hidden, "norm_gain": norm_gain, "w_query": w_query, "w_key": w_key, "w_value": w_value, "q_gain": q_gain, "k_gain": k_gain, "lengths": lengths, "piece_map": piece_map, "owner": owner, "slot": slot}


EPSILON = 1e-06
THETA = 1000000.0
NEG_BIG = -1e+30

def norm_rope(projected, gain_vec, relative, head_size):
    row_count = projected.shape[0]
    head_count = projected.shape[1] // head_size
    shaped = projected.reshape(row_count, head_count, head_size)
    factor = lax.rsqrt(lax.optimization_barrier(jnp.mean(shaped * shaped, axis=-1, keepdims=True)) + EPSILON)
    normal = shaped * factor * gain_vec
    half_size = head_size // 2
    frequency = jnp.exp(jnp.arange(half_size, dtype=jnp.float32) * (-2.0 * math.log(THETA) / head_size))
    angles = relative.astype(jnp.float32)[:, None] * frequency[None, :]
    cosine = jnp.cos(angles)[:, None, :]
    sine_part = jnp.sin(angles)[:, None, :]
    first_half = normal[..., :half_size]
    second = normal[..., half_size:]
    turned = jnp.concatenate([first_half * cosine - second * sine_part, second * cosine + first_half * sine_part], axis=-1)
    return turned.reshape(row_count, head_count * head_size).astype(jnp.bfloat16)

def reference(hidden, norm_gain, w_query, w_key, w_value, q_gain, k_gain, lengths, piece_map, owner, slot):
    inputs = hidden.astype(jnp.float32)
    factor = lax.rsqrt(lax.optimization_barrier(jnp.mean(inputs * inputs, axis=-1, keepdims=True)) + EPSILON)
    normed = (inputs * factor * norm_gain).astype(jnp.bfloat16)
    flat_rows = normed.reshape(-1, MODEL_WIDTH)
    query_raw = jnp.dot(flat_rows, w_query, preferred_element_type=jnp.float32)
    key_raw = jnp.dot(flat_rows, w_key, preferred_element_type=jnp.float32)
    value_rows = jnp.dot(flat_rows, w_value, preferred_element_type=jnp.float32).astype(jnp.bfloat16)
    pieces = jnp.transpose(piece_map).astype(jnp.int32)
    positions = pieces[:, :, None] * TOK_DEV + jnp.arange(TOK_DEV, dtype=jnp.int32)[None, None, :]
    seg_ends = jnp.cumsum(lengths, axis=1, dtype=jnp.int32)
    starts = seg_ends - lengths
    segment = lax.optimization_barrier(jnp.sum((positions[..., None] >= seg_ends[None, :, None, :]).astype(jnp.int32), axis=-1, dtype=jnp.int32))
    seg_ids = jnp.arange(NSEG, dtype=jnp.int32)
    relative = positions - lax.optimization_barrier(jnp.sum(jnp.where(segment[..., None] == seg_ids, starts[None, :, None, :], 0), axis=-1, dtype=jnp.int32))
    query_rows = norm_rope(query_raw, q_gain, relative.reshape(-1), HEAD_WIDTH)
    key_rows = norm_rope(key_raw, k_gain, relative.reshape(-1), HEAD_WIDTH)
    cache_index = (owner.reshape(-1) * CAP + slot.reshape(-1)).astype(jnp.int32)
    cache = jnp.zeros((OWNERS * CAP, 2 * KW), jnp.bfloat16).at[cache_index].set(jnp.concatenate([key_rows, value_rows], axis=1))

    def by_group(array, width):
        return jnp.swapaxes(array.reshape(PIECES, GROUPS, TOK_DEV, width), 0, 1).reshape(GROUPS, STREAM_TOKENS, width)
    group_pos = jnp.swapaxes(positions, 0, 1).reshape(GROUPS, STREAM_TOKENS)
    group_seg = jnp.swapaxes(segment, 0, 1).reshape(GROUPS, STREAM_TOKENS)
    rows_per_block = 512 if STREAM_TOKENS % 512 == 0 else STREAM_TOKENS
    group_width = QUERY_HEADS // KEY_VALUE_HEADS
    scale_factor = 1.0 / math.sqrt(HEAD_WIDTH)

    def one_group(operands):
        query_group, grouped_keys, grouped_values, pos_group, seg_group = operands
        heads_of_key = grouped_keys.reshape(STREAM_TOKENS, KEY_VALUE_HEADS, HEAD_WIDTH).astype(jnp.float32)
        heads_of_value = grouped_values.reshape(STREAM_TOKENS, KEY_VALUE_HEADS, HEAD_WIDTH).astype(jnp.float32)

        def one_block(block_in):
            block_of_query, pos_block, seg_block = block_in
            heads_of_query = block_of_query.reshape(rows_per_block, KEY_VALUE_HEADS, group_width, HEAD_WIDTH).astype(jnp.float32)
            scores = jnp.einsum('tkgd,skd->tkgs', heads_of_query, heads_of_key) * scale_factor
            visible = (seg_block[:, None] == seg_group[None, :]) & (pos_group[None, :] <= pos_block[:, None])
            visible = visible[:, None, None, :]
            masked = jnp.where(visible, scores, NEG_BIG)
            row_max = lax.optimization_barrier(jnp.max(masked, axis=-1, keepdims=True))
            weights = jnp.where(visible, jnp.exp(masked - row_max), 0.0)
            row_sum = lax.optimization_barrier(jnp.sum(weights, axis=-1))
            rounded = weights.astype(jnp.bfloat16).astype(jnp.float32)
            mixed = jnp.einsum('tkgs,skd->tkgd', rounded, heads_of_value) / row_sum[..., None]
            return mixed.reshape(rows_per_block, QW).astype(jnp.bfloat16)
        return lax.map(one_block, (query_group.reshape(-1, rows_per_block, QW), pos_group.reshape(-1, rows_per_block), seg_group.reshape(-1, rows_per_block)))
    outputs = lax.map(one_group, (by_group(query_rows, QW), by_group(key_rows, KW), by_group(value_rows, KW), group_pos, group_seg))
    attended = jnp.swapaxes(outputs.reshape(GROUPS, PIECES, TOK_DEV, QW), 0, 1)
    return (attended, cache)
```

```python
import functools
import math

import jax
import jax.numpy as jnp
from jax import lax
from jax.experimental import pallas as pl
from jax.experimental.pallas import tpu as pltpu
from jax.sharding import PartitionSpec as P

HEAD_WIDTH = 128
EPSILON = 1e-06
THETA = 1000000.0
NEG_BIG = -1e30
MESH = pl.DeviceIdType.MESH
LINE = 4
CORES = 2
BF = jnp.bfloat16
F32 = jnp.float32


def dot_nt(a, b):
    return lax.dot_general(a, b, (((1,), (1,)), ((), ())), preferred_element_type=F32)


def aligned(index, size):
    return pl.multiple_of(index * size, size)


def kernel(
    ctx_n, fsdp_n, seg_n,
    lengths, pieces, hidden, norm_gain, w_q, w_k, w_v, q_gain, k_gain, owner, slot,
    attended_out, cache_out,
    normed, wkv, wq, tab, cos_t, sin_t, kv, q_rows, bucket, got, slot2d, slot_msg, slot_got,
    attn, attn_got,
    w_send, w_recv, h_send, h_recv, f_send, t_send, t_recv,
    c_send, c_recv, s_send, s_recv, a_send, a_recv,
):
    ctx = lax.axis_index("ctx")
    fs = lax.axis_index("fsdp")
    me = ctx * fsdp_n + fs
    total_n = ctx_n * fsdp_n
    tok = hidden.shape[0]
    wide = w_q.shape[0]
    kc = w_k.shape[1]
    qc = w_q.shape[1]
    per = got.shape[1] // fsdp_n
    most = per // ctx_n
    minor_n = fsdp_n // LINE
    rows_y = ctx_n // CORES
    major, minor = fs // minor_n, fs % minor_n
    y_at, core = ctx // CORES, ctx % CORES
    sibling = y_at * CORES + (1 - core)

    barrier = pltpu.get_barrier_semaphore()

    @pl.loop(1, total_n)
    def _(step):
        other = (me + step) % total_n
        pl.semaphore_signal(
            barrier, inc=1, device_id=(other // fsdp_n, other % fsdp_n), device_id_type=MESH
        )

    wkv[pl.ds(aligned(fs, wide), wide), 0:kc] = w_k[...]
    wkv[pl.ds(aligned(fs, wide), wide), kc : 2 * kc] = w_v[...]
    wq[pl.ds(aligned(fs, wide), wide), :] = w_q[...]
    tab[ctx] = jnp.concatenate(
        [owner[...], slot[...], jnp.zeros((6, tok), jnp.int32)], axis=0
    )
    pl.semaphore_wait(barrier, total_n - 1)

    buffers = (wkv, wq)

    def w_copy(part, target, shard):
        spot = buffers[part].at[pl.ds(aligned(shard, wide), wide), :]
        to = ((fs + minor_n) % fsdp_n, (fs + fsdp_n - minor_n) % fsdp_n)[target] if target < 2 else (
            major * minor_n + (minor + target - 1) % minor_n
        )
        return pltpu.make_async_remote_copy(
            src_ref=spot, dst_ref=spot,
            send_sem=w_send.at[part, target, shard], recv_sem=w_recv.at[part, shard],
            device_id=(ctx, to), device_id_type=MESH,
        )

    def w_minors(part, shard):
        for target in range(2, minor_n + 1):
            w_copy(part, target, shard).start()

    def w_own(part):
        @pl.when(major < LINE - 1)
        def _():
            w_copy(part, 0, fs).start()

        @pl.when(major > 0)
        def _():
            w_copy(part, 1, fs).start()

        w_minors(part, fs)

    def w_step(part, k):
        @pl.when(major - k >= 0)
        def _():
            shard = fs - k * minor_n
            w_copy(part, 0, shard).wait_recv()

            @pl.when(major < LINE - 1)
            def _():
                w_copy(part, 0, shard).start()

            w_minors(part, shard)

        @pl.when(major + k < LINE)
        def _():
            shard = fs + k * minor_n
            w_copy(part, 1, shard).wait_recv()

            @pl.when(major > 0)
            def _():
                w_copy(part, 1, shard).start()

            w_minors(part, shard)

    def w_finish(part):
        for step in range(1, minor_n):
            for line in range(LINE):
                w_copy(part, 0, line * minor_n + (minor + step) % minor_n).wait_recv()

    def w_sent(part):
        for line in range(LINE):
            shard = line * minor_n + minor

            @pl.when((major < LINE - 1) & (line <= major))
            def _():
                w_copy(part, 0, shard).wait_send()

            @pl.when((major > 0) & (line >= major))
            def _():
                w_copy(part, 1, shard).wait_send()

            for target in range(2, minor_n + 1):
                w_copy(part, target, shard).wait_send()

    def h_copy(block, to, send_sem):
        spot = normed.at[pl.ds(aligned(block, tok), tok), :]
        return pltpu.make_async_remote_copy(
            src_ref=spot, dst_ref=spot, send_sem=send_sem, recv_sem=h_recv.at[block],
            device_id=(to, fs), device_id_type=MESH,
        )

    def t_copy(block, to):
        return pltpu.make_async_remote_copy(
            src_ref=tab.at[block], dst_ref=tab.at[block],
            send_sem=t_send.at[to], recv_sem=t_recv.at[block],
            device_id=(to, fs), device_id_type=MESH,
        )

    def across(step):
        return ((y_at + step) % rows_y) * CORES + core

    w_own(0)
    inputs = hidden[...].astype(F32)
    factor = lax.rsqrt(jnp.mean(inputs * inputs, axis=-1, keepdims=True) + EPSILON)
    normed[pl.ds(aligned(ctx, tok), tok), :] = (inputs * factor * norm_gain[...]).astype(BF)
    for step in range(1, rows_y):
        h_copy(ctx, across(step), h_send.at[step]).start()
    h_copy(ctx, sibling, h_send.at[0]).start()
    w_own(1)
    for step in range(1, ctx_n):
        t_copy(ctx, (ctx + step) % ctx_n).start()

    ends = []
    running = jnp.int32(0)
    for j in range(seg_n):
        running = running + lengths[fs, j]
        ends.append(running)

    def first_place(pos):
        first = jnp.zeros_like(pos)
        for end in ends:
            first = jnp.where(pos >= end, end, first)
        return first

    lane = lax.broadcasted_iota(jnp.int32, (1, HEAD_WIDTH), 1)
    half = HEAD_WIDTH // 2
    frequency = jnp.exp(
        (lane % half).astype(F32) * (-2.0 * math.log(THETA) / HEAD_WIDTH)
    )

    @pl.loop(0, ctx_n)
    def _(c):
        pos = lax.broadcasted_iota(jnp.int32, (tok, HEAD_WIDTH), 0) + pieces[fs, c] * tok
        angles = (pos - first_place(pos)).astype(F32) * frequency
        sine = jnp.sin(angles)
        at = pl.ds(aligned(c, tok), tok)
        cos_t[at, :] = jnp.cos(angles)
        sin_t[at, :] = jnp.where(lane < half, -sine, sine)

    for k in range(1, LINE):
        w_step(0, k)
        w_step(1, k)
        if k == 1:
            for step in range(1, rows_y):
                block = across(step)
                h_copy(block, sibling, h_send.at[0]).wait_recv()
                h_copy(block, sibling, f_send.at[block]).start()
    for step in range(1, ctx_n):
        t_copy((ctx + step) % ctx_n, ctx).wait_recv()

    owners = lax.broadcasted_iota(jnp.int32, (total_n, tok), 0)
    before = jnp.where(
        lax.broadcasted_iota(jnp.int32, (tok, tok), 0)
        < lax.broadcasted_iota(jnp.int32, (tok, tok), 1),
        1.0, 0.0,
    ).astype(BF)
    lane_shift = (fs * per) % HEAD_WIDTH
    places = []
    slots = jnp.zeros((total_n, HEAD_WIDTH), F32)
    for c in range(ctx_n):
        owner_row = tab[c, 0:1, :]
        slot_row = tab[c, 1:2, :] + 1
        mine = jnp.where(owners == owner_row, 1.0, 0.0)
        earlier = jnp.dot(mine.astype(BF), before, preferred_element_type=F32)
        rank = jnp.sum(mine * earlier, axis=0, keepdims=True).astype(jnp.int32)
        places.append(owner_row * per + c * most + rank)
        column = rank + (c * most + lane_shift)
        spread = jnp.where(
            lax.broadcasted_iota(jnp.int32, (HEAD_WIDTH, tok), 0) == column, 1.0, 0.0
        ).astype(BF)
        high = (mine * (slot_row // 32).astype(F32)).astype(BF)
        low = (mine * (slot_row % 32).astype(F32)).astype(BF)
        slots = slots + dot_nt(high, spread) * 32.0 + dot_nt(low, spread)
    place_row = jnp.concatenate(places, axis=1)
    slot2d[...] = slots

    @pl.loop(0, total_n)
    def _(o):
        slot_msg[o] = jnp.broadcast_to(slot2d[pl.ds(o, 1), :], (8, HEAD_WIDTH))

    w_finish(0)
    h_copy(sibling, sibling, h_send.at[0]).wait_recv()
    for step in range(1, rows_y):
        h_copy(((y_at + step) % rows_y) * CORES + 1 - core, sibling, h_send.at[0]).wait_recv()

    def norm_rope(x, gain, cosine, sine):
        scale = lax.rsqrt(jnp.mean(x * x, axis=-1, keepdims=True) + EPSILON)
        y = x * scale * gain
        return (y * cosine + pltpu.roll(y, half, 1) * sine).astype(BF)

    @pl.loop(0, ctx_n)
    def _(c):
        at = pl.ds(aligned(c, tok), tok)
        raw = jnp.dot(normed[at, :], wkv[...], preferred_element_type=F32)
        cosine, sine = cos_t[at, :], sin_t[at, :]
        for h in range(kc // HEAD_WIDTH):
            cols = slice(h * HEAD_WIDTH, (h + 1) * HEAD_WIDTH)
            kv[at, cols] = norm_rope(raw[:, cols], k_gain[...], cosine, sine)
        kv[at, kc : 2 * kc] = raw[:, kc:].astype(BF)

    chunk = 256

    @pl.loop(0, total_n * per // chunk)
    def _(i):
        rows = lax.broadcasted_iota(jnp.int32, (chunk, ctx_n * tok), 0) + i * chunk
        pick = jnp.where(rows == place_row, 1.0, 0.0).astype(BF)
        bucket[pl.ds(aligned(i, chunk), chunk), :] = jnp.dot(
            pick, kv[...], preferred_element_type=F32
        ).astype(BF)

    def c_copy(to, sender):
        return pltpu.make_async_remote_copy(
            src_ref=bucket.at[pl.ds(aligned(to, per), per), :],
            dst_ref=got.at[sender // fsdp_n, pl.ds(aligned(sender % fsdp_n, per), per), :],
            send_sem=c_send.at[to], recv_sem=c_recv.at[sender],
            device_id=(to // fsdp_n, to % fsdp_n), device_id_type=MESH,
        )

    def s_copy(to, sender):
        return pltpu.make_async_remote_copy(
            src_ref=slot_msg.at[to], dst_ref=slot_got.at[sender],
            send_sem=s_send.at[to], recv_sem=s_recv.at[sender],
            device_id=(to // fsdp_n, to % fsdp_n), device_id_type=MESH,
        )

    @pl.loop(1, total_n)
    def _(step):
        to = (me + step) % total_n
        c_copy(to, me).start()

        @pl.when(ctx == 0)
        def _():
            s_copy(to, fs).start()

    got[ctx, pl.ds(aligned(fs, per), per), :] = bucket[pl.ds(aligned(me, per), per), :]

    @pl.when(ctx == 0)
    def _():
        slot_got[fs] = slot_msg[me]

    w_finish(1)

    @pl.loop(0, ctx_n)
    def _(c):
        at = pl.ds(aligned(c, tok), tok)
        raw = jnp.dot(normed[at, :], wq[...], preferred_element_type=F32)
        cosine, sine = cos_t[at, :], sin_t[at, :]
        for h in range(qc // HEAD_WIDTH):
            cols = slice(h * HEAD_WIDTH, (h + 1) * HEAD_WIDTH)
            q_rows[at, cols] = norm_rope(raw[:, cols], q_gain[...], cosine, sine)

    key_pos = jnp.concatenate(
        [
            lax.broadcasted_iota(jnp.int32, (1, tok), 1) + pieces[fs, c] * tok
            for c in range(ctx_n)
        ],
        axis=1,
    )

    def a_copy(block, sender):
        return pltpu.make_async_remote_copy(
            src_ref=attn.at[pl.ds(aligned(block, tok), tok), :], dst_ref=attn_got.at[sender],
            send_sem=a_send.at[block], recv_sem=a_recv.at[sender],
            device_id=(block, fs), device_id_type=MESH,
        )

    group_width = qc // kc

    @pl.loop(0, ctx_n)
    def _(step):
        c = (ctx + 1 + step) % ctx_n
        at = pl.ds(aligned(c, tok), tok)
        pos = lax.broadcasted_iota(jnp.int32, (tok, 1), 0) + pieces[fs, c] * tok
        visible = (key_pos <= pos) & (key_pos >= first_place(pos))
        for h in range(qc // HEAD_WIDTH):
            j = h // group_width
            cols = slice(h * HEAD_WIDTH, (h + 1) * HEAD_WIDTH)
            keys = kv[:, j * HEAD_WIDTH : (j + 1) * HEAD_WIDTH]
            values = kv[:, kc + j * HEAD_WIDTH : kc + (j + 1) * HEAD_WIDTH]
            scores = dot_nt(q_rows[at, cols], keys) * (1.0 / math.sqrt(HEAD_WIDTH))
            masked = jnp.where(visible, scores, NEG_BIG)
            weights = jnp.exp(masked - jnp.max(masked, axis=-1, keepdims=True))
            total = jnp.sum(weights, axis=-1, keepdims=True)
            mixed = jnp.dot(weights.astype(BF), values, preferred_element_type=F32)
            attn[at, cols] = (mixed / total).astype(BF)

        @pl.when(step < ctx_n - 1)
        def _():
            a_copy(c, ctx).start()

    attn_got[ctx] = attn[pl.ds(aligned(ctx, tok), tok), :]

    for g in range(fsdp_n):
        @pl.when((ctx > 0) | (fs != g))
        def _():
            s_copy(me, g).wait_recv()

    shared = HEAD_WIDTH // per
    slot_line = jnp.concatenate(
        [
            sum(slot_got[p * shared + i, 0:1, :] for i in range(shared))
            for p in range(fsdp_n // shared)
        ],
        axis=1,
    )
    cap = cache_out.shape[0]
    place = jnp.where(
        lax.broadcasted_iota(jnp.int32, (cap, fsdp_n * per), 0) + 1
        == slot_line.astype(jnp.int32),
        1.0, 0.0,
    ).astype(BF)

    for step in range(1, ctx_n):
        a_copy(ctx, (ctx + step) % ctx_n).wait_recv()
    for c in range(ctx_n):
        attended_out[:, c * qc : (c + 1) * qc] = attn_got[c]

    @pl.loop(1, total_n)
    def _(step):
        c_copy(me, (me + step) % total_n).wait_recv()

    for c in range(ctx_n):
        rows = jnp.dot(place, got[c], preferred_element_type=F32).astype(BF)
        cache_out[:, c * kc : (c + 1) * kc] = rows[:, :kc]
        cache_out[:, (ctx_n + c) * kc : (ctx_n + c + 1) * kc] = rows[:, kc:]

    w_sent(0)
    w_sent(1)
    for step in range(1, rows_y):
        h_copy(ctx, across(step), h_send.at[step]).wait_send()
        block = across(step)
        h_copy(block, sibling, f_send.at[block]).wait_send()
    h_copy(ctx, sibling, h_send.at[0]).wait_send()
    for step in range(1, ctx_n):
        t_copy(ctx, (ctx + step) % ctx_n).wait_send()
        a_copy((ctx + step) % ctx_n, ctx).wait_send()

    @pl.loop(1, total_n)
    def _(step):
        to = (me + step) % total_n
        c_copy(to, me).wait_send()

        @pl.when(ctx == 0)
        def _():
            s_copy(to, fs).wait_send()


def shards(
    ctx_n, fsdp_n,
    hidden, norm_gain, w_query, w_key, w_value, q_gain, k_gain, lengths, piece_map, owner, slot,
):
    tok, width = hidden.shape[2:]
    kc, qc = w_key.shape[1], w_query.shape[1]
    total_n = ctx_n * fsdp_n
    most = 2 * tok // total_n
    per = ctx_n * most
    stream = ctx_n * tok
    minor_n = fsdp_n // LINE
    vmem = pl.BlockSpec(memory_space=pltpu.VMEM)
    smem = pl.BlockSpec(memory_space=pltpu.SMEM)
    dma = pltpu.SemaphoreType.DMA
    attended, cache = pl.pallas_call(
        functools.partial(kernel, ctx_n, fsdp_n, lengths.shape[1]),
        out_shape=(
            jax.ShapeDtypeStruct((tok, ctx_n * qc), BF),
            jax.ShapeDtypeStruct((total_n * most, 2 * ctx_n * kc), BF),
        ),
        in_specs=[smem, smem] + [vmem] * 9,
        out_specs=(vmem, vmem),
        scratch_shapes=[
            pltpu.VMEM((stream, width), BF),
            pltpu.VMEM((width, 2 * kc), BF),
            pltpu.VMEM((width, qc), BF),
            pltpu.VMEM((ctx_n, 8, tok), jnp.int32),
            pltpu.VMEM((stream, HEAD_WIDTH), F32),
            pltpu.VMEM((stream, HEAD_WIDTH), F32),
            pltpu.VMEM((stream, 2 * kc), BF),
            pltpu.VMEM((stream, qc), BF),
            pltpu.VMEM((total_n * per, 2 * kc), BF),
            pltpu.VMEM((ctx_n, fsdp_n * per, 2 * kc), BF),
            pltpu.VMEM((total_n, HEAD_WIDTH), F32),
            pltpu.VMEM((total_n, 8, HEAD_WIDTH), F32),
            pltpu.VMEM((fsdp_n, 8, HEAD_WIDTH), F32),
            pltpu.VMEM((stream, qc), BF),
            pltpu.VMEM((ctx_n, tok, qc), BF),
            dma((2, minor_n + 1, fsdp_n)),
            dma((2, fsdp_n)),
            dma((ctx_n,)),
            dma((ctx_n,)),
            dma((ctx_n,)),
            dma((ctx_n,)),
            dma((ctx_n,)),
            dma((total_n,)),
            dma((total_n,)),
            dma((total_n,)),
            dma((fsdp_n,)),
            dma((ctx_n,)),
            dma((ctx_n,)),
        ],
        compiler_params=pltpu.CompilerParams(
            collective_id=0, has_side_effects=True, vmem_limit_bytes=56 * 1024 * 1024
        ),
        name="prefill",
    )(
        lengths, piece_map, hidden[0, 0], norm_gain[None], w_query, w_key, w_value,
        q_gain[None], k_gain[None], owner[0], slot[0],
    )
    return (attended[None, None], cache)


def solution(mesh):
    placed = (
        P("ctx", "fsdp", None, None),
        P(),
        P("fsdp", "ctx"),
        P("fsdp", "ctx"),
        P("fsdp", "ctx"),
        P(),
        P(),
        P(),
        P(),
        P("ctx", "fsdp", None),
        P("ctx", "fsdp", None),
    )
    return jax.shard_map(
        functools.partial(shards, mesh.shape["ctx"], mesh.shape["fsdp"]),
        mesh=mesh,
        in_specs=placed,
        out_specs=(P("ctx", "fsdp", None, None), P(("ctx", "fsdp"), None)),
        check_vma=False,
    )
```

```python
import functools
import math

import jax
import jax.numpy as jnp
from jax import lax
from jax.experimental import pallas as pl
from jax.experimental.pallas import tpu as pltpu
from jax.sharding import PartitionSpec as P

HEAD_WIDTH = 128
EPSILON = 1e-06
THETA = 1000000.0
NEG_BIG = -1e30
MESH = pl.DeviceIdType.MESH
LINE = 4
CORES = 2
BF = jnp.bfloat16
F32 = jnp.float32


def dot_nt(a, b):
    return lax.dot_general(a, b, (((1,), (1,)), ((), ())), preferred_element_type=F32)


def aligned(index, size):
    return pl.multiple_of(index * size, size)


def kernel(
    ctx_n, fsdp_n, seg_n,
    lengths, pieces, hidden, norm_gain, w_q, w_k, w_v, q_gain, k_gain, owner, slot,
    attn_out, got_out, line_out,
    normed, wkv, wq, tab, cos_t, sin_t, kv, q_rows, bucket, got, slot2d, slot_msg, slot_got,
    attn, attn_got,
    w_send, w_recv, h_send, h_recv, f_send, t_send, t_recv,
    c_send, c_recv, s_send, s_recv, a_send, a_recv, o_sem,
):
    ctx = lax.axis_index("ctx")
    fs = lax.axis_index("fsdp")
    me = ctx * fsdp_n + fs
    total_n = ctx_n * fsdp_n
    tok = hidden.shape[0]
    wide = w_q.shape[0]
    kc = w_k.shape[1]
    qc = w_q.shape[1]
    per = got.shape[1] // fsdp_n
    most = per // ctx_n
    minor_n = fsdp_n // LINE
    rows_y = ctx_n // CORES
    major, minor = fs // minor_n, fs % minor_n
    y_at, core = ctx // CORES, ctx % CORES
    sibling = y_at * CORES + (1 - core)

    barrier = pltpu.get_barrier_semaphore()

    @pl.loop(1, total_n)
    def _(step):
        other = (me + step) % total_n
        pl.semaphore_signal(
            barrier, inc=1, device_id=(other // fsdp_n, other % fsdp_n), device_id_type=MESH
        )

    wkv[pl.ds(aligned(fs, wide), wide), 0:kc] = w_k[...]
    wkv[pl.ds(aligned(fs, wide), wide), kc : 2 * kc] = w_v[...]
    wq[pl.ds(aligned(fs, wide), wide), :] = w_q[...]
    tab[ctx] = jnp.concatenate(
        [owner[...], slot[...], jnp.zeros((6, tok), jnp.int32)], axis=0
    )
    pl.semaphore_wait(barrier, total_n - 1)

    buffers = (wkv, wq)

    def w_copy(part, target, shard):
        spot = buffers[part].at[pl.ds(aligned(shard, wide), wide), :]
        to = ((fs + minor_n) % fsdp_n, (fs + fsdp_n - minor_n) % fsdp_n)[target] if target < 2 else (
            major * minor_n + (minor + target - 1) % minor_n
        )
        return pltpu.make_async_remote_copy(
            src_ref=spot, dst_ref=spot,
            send_sem=w_send.at[part, target, shard], recv_sem=w_recv.at[part, shard],
            device_id=(ctx, to), device_id_type=MESH,
        )

    def w_minors(part, shard):
        for target in range(2, minor_n + 1):
            w_copy(part, target, shard).start()

    def w_own(part):
        @pl.when(major < LINE - 1)
        def _():
            w_copy(part, 0, fs).start()

        @pl.when(major > 0)
        def _():
            w_copy(part, 1, fs).start()

        w_minors(part, fs)

    def w_step(part, k):
        @pl.when(major - k >= 0)
        def _():
            shard = fs - k * minor_n
            w_copy(part, 0, shard).wait_recv()

            @pl.when(major < LINE - 1)
            def _():
                w_copy(part, 0, shard).start()

            w_minors(part, shard)

        @pl.when(major + k < LINE)
        def _():
            shard = fs + k * minor_n
            w_copy(part, 1, shard).wait_recv()

            @pl.when(major > 0)
            def _():
                w_copy(part, 1, shard).start()

            w_minors(part, shard)

    def w_finish(part):
        for step in range(1, minor_n):
            for line in range(LINE):
                w_copy(part, 0, line * minor_n + (minor + step) % minor_n).wait_recv()

    def w_sent(part):
        for line in range(LINE):
            shard = line * minor_n + minor

            @pl.when((major < LINE - 1) & (line <= major))
            def _():
                w_copy(part, 0, shard).wait_send()

            @pl.when((major > 0) & (line >= major))
            def _():
                w_copy(part, 1, shard).wait_send()

            for target in range(2, minor_n + 1):
                w_copy(part, target, shard).wait_send()

    def h_copy(block, to, send_sem):
        spot = normed.at[pl.ds(aligned(block, tok), tok), :]
        return pltpu.make_async_remote_copy(
            src_ref=spot, dst_ref=spot, send_sem=send_sem, recv_sem=h_recv.at[block],
            device_id=(to, fs), device_id_type=MESH,
        )

    def t_copy(block, to):
        return pltpu.make_async_remote_copy(
            src_ref=tab.at[block], dst_ref=tab.at[block],
            send_sem=t_send.at[to], recv_sem=t_recv.at[block],
            device_id=(to, fs), device_id_type=MESH,
        )

    def across(step):
        return ((y_at + step) % rows_y) * CORES + core

    w_own(0)
    inputs = hidden[...].astype(F32)
    factor = lax.rsqrt(jnp.mean(inputs * inputs, axis=-1, keepdims=True) + EPSILON)
    normed[pl.ds(aligned(ctx, tok), tok), :] = (inputs * factor * norm_gain[...]).astype(BF)
    for step in range(1, rows_y):
        h_copy(ctx, across(step), h_send.at[step]).start()
    h_copy(ctx, sibling, h_send.at[0]).start()
    for step in range(1, ctx_n):
        t_copy(ctx, (ctx + step) % ctx_n).start()

    def entry(table, column):
        at = (lax.broadcasted_iota(jnp.int32, table.shape, 0) == column) & (
            lax.broadcasted_iota(jnp.int32, table.shape, 1) == fs
        )
        row = jnp.sum(jnp.where(at, table[...].astype(F32), 0.0), axis=0, keepdims=True)
        return jnp.sum(row, axis=1, keepdims=True).astype(jnp.int32)

    ends = []
    running = jnp.zeros((1, 1), jnp.int32)
    for j in range(seg_n):
        running = running + entry(lengths, j)
        ends.append(running)

    def first_place(pos):
        first = jnp.zeros_like(pos)
        for end in ends:
            first = jnp.where(pos >= end, end, first)
        return first

    lane = lax.broadcasted_iota(jnp.int32, (1, HEAD_WIDTH), 1)
    half = HEAD_WIDTH // 2
    frequency = jnp.exp(
        (lane % half).astype(F32) * (-2.0 * math.log(THETA) / HEAD_WIDTH)
    )

    def rope_tables(first, last):
        @pl.loop(first, last)
        def _(c):
            pos = lax.broadcasted_iota(jnp.int32, (tok, HEAD_WIDTH), 0) + entry(pieces, c) * tok
            angles = (pos - first_place(pos)).astype(F32) * frequency
            sine = jnp.sin(angles)
            at = pl.ds(aligned(c, tok), tok)
            cos_t[at, :] = jnp.cos(angles)
            sin_t[at, :] = jnp.where(lane < half, -sine, sine)

    w_step(0, 1)
    w_own(1)
    rope_tables(0, ctx_n // 2)
    w_step(0, 2)
    rope_tables(ctx_n // 2, ctx_n)
    w_step(0, 3)
    w_step(1, 1)
    for step in range(1, ctx_n):
        t_copy((ctx + step) % ctx_n, ctx).wait_recv()

    owners = lax.broadcasted_iota(jnp.int32, (total_n, tok), 0)
    before = jnp.where(
        lax.broadcasted_iota(jnp.int32, (tok, tok), 0)
        < lax.broadcasted_iota(jnp.int32, (tok, tok), 1),
        1.0, 0.0,
    ).astype(BF)
    lane_shift = (fs * per) % HEAD_WIDTH
    places = []
    slots = jnp.zeros((total_n, HEAD_WIDTH), F32)
    for c in range(ctx_n):
        owner_row = tab[c, 0:1, :]
        slot_row = tab[c, 1:2, :] + 1
        mine = jnp.where(owners == owner_row, 1.0, 0.0)
        earlier = jnp.dot(mine.astype(BF), before, preferred_element_type=F32)
        rank = jnp.sum(mine * earlier, axis=0, keepdims=True).astype(jnp.int32)
        places.append(owner_row * per + c * most + rank)
        column = rank + (c * most + lane_shift)
        spread = jnp.where(
            lax.broadcasted_iota(jnp.int32, (HEAD_WIDTH, tok), 0) == column, 1.0, 0.0
        ).astype(BF)
        high = (mine * (slot_row // 32).astype(F32)).astype(BF)
        low = (mine * (slot_row % 32).astype(F32)).astype(BF)
        slots = slots + dot_nt(high, spread) * 32.0 + dot_nt(low, spread)
    place_row = jnp.concatenate(places, axis=1)
    slot2d[...] = slots

    @pl.loop(0, total_n)
    def _(o):
        slot_msg[o] = jnp.broadcast_to(slot2d[pl.ds(o, 1), :], (8, HEAD_WIDTH))

    for step in range(1, rows_y):
        block = across(step)
        h_copy(block, sibling, h_send.at[0]).wait_recv()
        h_copy(block, sibling, f_send.at[block]).start()
    w_step(1, 2)
    w_finish(0)
    h_copy(sibling, sibling, h_send.at[0]).wait_recv()
    for step in range(1, rows_y):
        h_copy(((y_at + step) % rows_y) * CORES + 1 - core, sibling, h_send.at[0]).wait_recv()

    def norm_rope(x, gain, cosine, sine):
        scale = lax.rsqrt(jnp.mean(x * x, axis=-1, keepdims=True) + EPSILON)
        y = x * scale * gain
        return (y * cosine + pltpu.roll(y, half, 1) * sine).astype(BF)

    @pl.loop(0, ctx_n)
    def _(c):
        at = pl.ds(aligned(c, tok), tok)
        raw = jnp.dot(normed[at, :], wkv[...], preferred_element_type=F32)
        cosine, sine = cos_t[at, :], sin_t[at, :]
        for h in range(kc // HEAD_WIDTH):
            cols = slice(h * HEAD_WIDTH, (h + 1) * HEAD_WIDTH)
            kv[at, cols] = norm_rope(raw[:, cols], k_gain[...], cosine, sine)
        kv[at, kc : 2 * kc] = raw[:, kc:].astype(BF)

    def c_copy(to, sender):
        return pltpu.make_async_remote_copy(
            src_ref=bucket.at[pl.ds(aligned(to, per), per), :],
            dst_ref=got.at[sender // fsdp_n, pl.ds(aligned(sender % fsdp_n, per), per), :],
            send_sem=c_send.at[to], recv_sem=c_recv.at[sender],
            device_id=(to // fsdp_n, to % fsdp_n), device_id_type=MESH,
        )

    def s_copy(to, sender):
        return pltpu.make_async_remote_copy(
            src_ref=slot_msg.at[to], dst_ref=slot_got.at[sender],
            send_sem=s_send.at[to], recv_sem=s_recv.at[sender],
            device_id=(to // fsdp_n, to % fsdp_n), device_id_type=MESH,
        )

    chunk = 256
    chunks = total_n * per // chunk
    reach = chunk // per

    @pl.loop(0, chunks)
    def _(step):
        i = (me // reach + 1 + 2 * (step % (chunks // 2)) + step // (chunks // 2)) % chunks
        rows = lax.broadcasted_iota(jnp.int32, (chunk, ctx_n * tok), 0) + i * chunk
        pick = jnp.where(rows == place_row, 1.0, 0.0).astype(BF)
        bucket[pl.ds(aligned(i, chunk), chunk), :] = jnp.dot(
            pick, kv[...], preferred_element_type=F32
        ).astype(BF)

        @pl.loop(0, reach)
        def _(inner):
            to = i * reach + (me + inner) % reach

            @pl.when(to != me)
            def _():
                c_copy(to, me).start()

                @pl.when(ctx == 0)
                def _():
                    s_copy(to, fs).start()

    got[ctx, pl.ds(aligned(fs, per), per), :] = bucket[pl.ds(aligned(me, per), per), :]

    @pl.when(ctx == 0)
    def _():
        slot_got[fs] = slot_msg[me]

    w_step(1, 3)
    w_finish(1)

    @pl.loop(0, ctx_n)
    def _(c):
        at = pl.ds(aligned(c, tok), tok)
        raw = jnp.dot(normed[at, :], wq[...], preferred_element_type=F32)
        cosine, sine = cos_t[at, :], sin_t[at, :]
        for h in range(qc // HEAD_WIDTH):
            cols = slice(h * HEAD_WIDTH, (h + 1) * HEAD_WIDTH)
            q_rows[at, cols] = norm_rope(raw[:, cols], q_gain[...], cosine, sine)

    key_pos = jnp.concatenate(
        [
            lax.broadcasted_iota(jnp.int32, (1, tok), 1) + entry(pieces, c) * tok
            for c in range(ctx_n)
        ],
        axis=1,
    )

    def a_copy(block, sender):
        return pltpu.make_async_remote_copy(
            src_ref=attn.at[pl.ds(aligned(block, tok), tok), :], dst_ref=attn_got.at[sender],
            send_sem=a_send.at[block], recv_sem=a_recv.at[sender],
            device_id=(block, fs), device_id_type=MESH,
        )

    group_width = qc // kc

    @pl.loop(0, ctx_n)
    def _(step):
        c = (ctx + 1 + step) % ctx_n
        at = pl.ds(aligned(c, tok), tok)
        pos = lax.broadcasted_iota(jnp.int32, (tok, 1), 0) + entry(pieces, c) * tok
        visible = (key_pos <= pos) & (key_pos >= first_place(pos))
        for h in range(qc // HEAD_WIDTH):
            j = h // group_width
            cols = slice(h * HEAD_WIDTH, (h + 1) * HEAD_WIDTH)
            keys = kv[:, j * HEAD_WIDTH : (j + 1) * HEAD_WIDTH]
            values = kv[:, kc + j * HEAD_WIDTH : kc + (j + 1) * HEAD_WIDTH]
            scores = dot_nt(q_rows[at, cols], keys) * (1.0 / math.sqrt(HEAD_WIDTH))
            masked = jnp.where(visible, scores, NEG_BIG)
            weights = jnp.exp(masked - jnp.max(masked, axis=-1, keepdims=True))
            total = jnp.sum(weights, axis=-1, keepdims=True)
            mixed = jnp.dot(weights.astype(BF), values, preferred_element_type=F32)
            attn[at, cols] = (mixed / total).astype(BF)

        @pl.when(step < ctx_n - 1)
        def _():
            a_copy(c, ctx).start()

    attn_got[ctx] = attn[pl.ds(aligned(ctx, tok), tok), :]

    for g in range(fsdp_n):
        @pl.when((ctx > 0) | (fs != g))
        def _():
            s_copy(me, g).wait_recv()

    shared = HEAD_WIDTH // per
    slot_line = jnp.concatenate(
        [
            sum(slot_got[p * shared + i, 0:1, :] for i in range(shared))
            for p in range(fsdp_n // shared)
        ],
        axis=1,
    )
    line_out[...] = jnp.broadcast_to(slot_line, line_out.shape)

    def out_copy(which, c):
        source, target = ((attn_got, attn_out), (got, got_out))[which]
        return pltpu.make_async_copy(source.at[c], target.at[c], o_sem.at[which, c])

    out_copy(0, ctx).start()
    for step in range(1, ctx_n):
        sender = (ctx + step) % ctx_n
        a_copy(ctx, sender).wait_recv()
        out_copy(0, sender).start()

    for step in range(ctx_n):
        sender = (ctx + step) % ctx_n

        @pl.loop(1 if step == 0 else 0, fsdp_n)
        def _(g):
            c_copy(me, sender * fsdp_n + (fs + g) % fsdp_n).wait_recv()

        out_copy(1, sender).start()

    w_sent(0)
    w_sent(1)
    for step in range(1, rows_y):
        h_copy(ctx, across(step), h_send.at[step]).wait_send()
        block = across(step)
        h_copy(block, sibling, f_send.at[block]).wait_send()
    h_copy(ctx, sibling, h_send.at[0]).wait_send()
    for step in range(1, ctx_n):
        t_copy(ctx, (ctx + step) % ctx_n).wait_send()
        a_copy((ctx + step) % ctx_n, ctx).wait_send()

    @pl.loop(1, total_n)
    def _(step):
        to = (me + step) % total_n
        c_copy(to, me).wait_send()

        @pl.when(ctx == 0)
        def _():
            s_copy(to, fs).wait_send()

    for c in range(ctx_n):
        out_copy(0, c).wait()
        out_copy(1, c).wait()


def place_rows(line, rows, heads, cache, attended, place):
    @pl.when((pl.program_id(0) == 0) & (pl.program_id(1) == 0))
    def _():
        spot = lax.broadcasted_iota(jnp.int32, place.shape, 0) + 1
        place[...] = jnp.where(spot == line[0:1, :].astype(jnp.int32), 1.0, 0.0).astype(BF)

    attended[...] = heads[0]
    cache[...] = jnp.dot(place[...], rows[0], preferred_element_type=F32).astype(BF)


def shards(
    ctx_n, fsdp_n,
    hidden, norm_gain, w_query, w_key, w_value, q_gain, k_gain, lengths, piece_map, owner, slot,
):
    tok, width = hidden.shape[2:]
    kc, qc = w_key.shape[1], w_query.shape[1]
    total_n = ctx_n * fsdp_n
    most = 2 * tok // total_n
    per = ctx_n * most
    stream = ctx_n * tok
    minor_n = fsdp_n // LINE
    vmem = pl.BlockSpec(memory_space=pltpu.VMEM)
    anywhere = pl.BlockSpec(memory_space=pl.ANY)
    dma = pltpu.SemaphoreType.DMA
    cap = total_n * most
    heads, got, line = pl.pallas_call(
        functools.partial(kernel, ctx_n, fsdp_n, lengths.shape[1]),
        out_shape=(
            jax.ShapeDtypeStruct((ctx_n, tok, qc), BF),
            jax.ShapeDtypeStruct((ctx_n, fsdp_n * per, 2 * kc), BF),
            jax.ShapeDtypeStruct((8, fsdp_n * per), F32),
        ),
        in_specs=[vmem] * 11,
        out_specs=(anywhere, anywhere, vmem),
        scratch_shapes=[
            pltpu.VMEM((stream, width), BF),
            pltpu.VMEM((width, 2 * kc), BF),
            pltpu.VMEM((width, qc), BF),
            pltpu.VMEM((ctx_n, 8, tok), jnp.int32),
            pltpu.VMEM((stream, HEAD_WIDTH), F32),
            pltpu.VMEM((stream, HEAD_WIDTH), F32),
            pltpu.VMEM((stream, 2 * kc), BF),
            pltpu.VMEM((stream, qc), BF),
            pltpu.VMEM((total_n * per, 2 * kc), BF),
            pltpu.VMEM((ctx_n, fsdp_n * per, 2 * kc), BF),
            pltpu.VMEM((total_n, HEAD_WIDTH), F32),
            pltpu.VMEM((total_n, 8, HEAD_WIDTH), F32),
            pltpu.VMEM((fsdp_n, 8, HEAD_WIDTH), F32),
            pltpu.VMEM((stream, qc), BF),
            pltpu.VMEM((ctx_n, tok, qc), BF),
            dma((2, minor_n + 1, fsdp_n)),
            dma((2, fsdp_n)),
            dma((ctx_n,)),
            dma((ctx_n,)),
            dma((ctx_n,)),
            dma((ctx_n,)),
            dma((ctx_n,)),
            dma((total_n,)),
            dma((total_n,)),
            dma((total_n,)),
            dma((fsdp_n,)),
            dma((ctx_n,)),
            dma((ctx_n,)),
            dma((2, ctx_n)),
        ],
        compiler_params=pltpu.CompilerParams(
            collective_id=0, has_side_effects=True, vmem_limit_bytes=56 * 1024 * 1024
        ),
        name="prefill",
    )(
        lengths.T, piece_map.T, hidden[0, 0], norm_gain[None], w_query, w_key, w_value,
        q_gain[None], k_gain[None], owner[0], slot[0],
    )
    cache, attended = pl.pallas_call(
        place_rows,
        out_shape=(
            jax.ShapeDtypeStruct((cap, 2 * ctx_n * kc), BF),
            jax.ShapeDtypeStruct((tok, ctx_n * qc), BF),
        ),
        grid=(2, ctx_n),
        in_specs=[
            pl.BlockSpec((8, fsdp_n * per), lambda half, c: (0, 0)),
            pl.BlockSpec((1, fsdp_n * per, kc), lambda half, c: (c, 0, half)),
            pl.BlockSpec((1, tok // 2, qc), lambda half, c: (c, half, 0)),
        ],
        out_specs=(
            pl.BlockSpec((cap, kc), lambda half, c: (0, half * ctx_n + c)),
            pl.BlockSpec((tok // 2, qc), lambda half, c: (half, c)),
        ),
        scratch_shapes=[pltpu.VMEM((cap, fsdp_n * per), BF)],
        compiler_params=pltpu.CompilerParams(vmem_limit_bytes=56 * 1024 * 1024),
        name="place_rows",
    )(line, got, heads)
    return (attended[None, None], cache)


def solution(mesh):
    placed = (
        P("ctx", "fsdp", None, None),
        P(),
        P("fsdp", "ctx"),
        P("fsdp", "ctx"),
        P("fsdp", "ctx"),
        P(),
        P(),
        P(),
        P(),
        P("ctx", "fsdp", None),
        P("ctx", "fsdp", None),
    )
    return jax.shard_map(
        functools.partial(shards, mesh.shape["ctx"], mesh.shape["fsdp"]),
        mesh=mesh,
        in_specs=placed,
        out_specs=(P("ctx", "fsdp", None, None), P(("ctx", "fsdp"), None)),
        check_vma=False,
    )
```

```python
import functools
import math

import jax
import jax.numpy as jnp
from jax import lax
from jax.experimental import pallas as pl
from jax.experimental.pallas import tpu as pltpu
from jax.sharding import PartitionSpec as P

HEAD_WIDTH = 128
EPSILON = 1e-06
THETA = 1000000.0
NEG_BIG = -1e30
EXPONENT = math.log2(math.e) / math.sqrt(HEAD_WIDTH)
MESH = pl.DeviceIdType.MESH
LINE = 4
CORES = 2
BF = jnp.bfloat16
F32 = jnp.float32


def dot_nt(a, b):
    return lax.dot_general(a, b, (((1,), (1,)), ((), ())), preferred_element_type=F32)


def aligned(index, size):
    return pl.multiple_of(index * size, size)


def kernel(
    ctx_n, fsdp_n, seg_n,
    lengths, pieces, hidden, norm_gain, w_q, w_k, w_v, q_gain, k_gain, owner, slot,
    attn_out, got_out, line_out,
    normed, wkv, wq, tab, cos_t, sin_t, kv, q_rows, bucket, got, slot2d, slot_msg, slot_got,
    attn, attn_got,
    w_send, w_recv, h_send, h_recv, f_send, t_send, t_recv,
    c_send, c_recv, s_send, s_recv, a_send, a_recv, o_sem,
):
    ctx = lax.axis_index("ctx")
    fs = lax.axis_index("fsdp")
    me = ctx * fsdp_n + fs
    total_n = ctx_n * fsdp_n
    tok = hidden.shape[0]
    wide = w_q.shape[0]
    kc = w_k.shape[1]
    qc = w_q.shape[1]
    per = got.shape[1] // fsdp_n
    most = per // ctx_n
    minor_n = fsdp_n // LINE
    rows_y = ctx_n // CORES
    major, minor = fs // minor_n, fs % minor_n
    y_at, core = ctx // CORES, ctx % CORES
    sibling = y_at * CORES + (1 - core)

    barrier = pltpu.get_barrier_semaphore()

    @pl.loop(1, total_n)
    def _(step):
        other = (me + step) % total_n
        pl.semaphore_signal(
            barrier, inc=1, device_id=(other // fsdp_n, other % fsdp_n), device_id_type=MESH
        )

    wkv[pl.ds(aligned(fs, wide), wide), 0:kc] = w_k[...]
    wkv[pl.ds(aligned(fs, wide), wide), kc : 2 * kc] = w_v[...]
    wq[pl.ds(aligned(fs, wide), wide), :] = w_q[...]
    tab[ctx] = jnp.concatenate(
        [owner[...], slot[...], jnp.zeros((6, tok), jnp.int32)], axis=0
    )
    pl.semaphore_wait(barrier, total_n - 1)

    buffers = (wkv, wq)

    def w_copy(part, target, shard):
        spot = buffers[part].at[pl.ds(aligned(shard, wide), wide), :]
        to = ((fs + minor_n) % fsdp_n, (fs + fsdp_n - minor_n) % fsdp_n)[target] if target < 2 else (
            major * minor_n + (minor + target - 1) % minor_n
        )
        return pltpu.make_async_remote_copy(
            src_ref=spot, dst_ref=spot,
            send_sem=w_send.at[part, target, shard], recv_sem=w_recv.at[part, shard],
            device_id=(ctx, to), device_id_type=MESH,
        )

    def w_minors(part, shard):
        for target in range(2, minor_n + 1):
            w_copy(part, target, shard).start()

    def w_own(part):
        @pl.when(major < LINE - 1)
        def _():
            w_copy(part, 0, fs).start()

        @pl.when(major > 0)
        def _():
            w_copy(part, 1, fs).start()

        w_minors(part, fs)

    def w_step(part, k):
        @pl.when(major - k >= 0)
        def _():
            shard = fs - k * minor_n
            w_copy(part, 0, shard).wait_recv()

            @pl.when(major < LINE - 1)
            def _():
                w_copy(part, 0, shard).start()

            w_minors(part, shard)

        @pl.when(major + k < LINE)
        def _():
            shard = fs + k * minor_n
            w_copy(part, 1, shard).wait_recv()

            @pl.when(major > 0)
            def _():
                w_copy(part, 1, shard).start()

            w_minors(part, shard)

    def w_finish(part):
        for step in range(1, minor_n):
            for line in range(LINE):
                w_copy(part, 0, line * minor_n + (minor + step) % minor_n).wait_recv()

    def w_sent(part):
        for line in range(LINE):
            shard = line * minor_n + minor

            @pl.when((major < LINE - 1) & (line <= major))
            def _():
                w_copy(part, 0, shard).wait_send()

            @pl.when((major > 0) & (line >= major))
            def _():
                w_copy(part, 1, shard).wait_send()

            for target in range(2, minor_n + 1):
                w_copy(part, target, shard).wait_send()

    def h_copy(block, to, send_sem):
        spot = normed.at[pl.ds(aligned(block, tok), tok), :]
        return pltpu.make_async_remote_copy(
            src_ref=spot, dst_ref=spot, send_sem=send_sem, recv_sem=h_recv.at[block],
            device_id=(to, fs), device_id_type=MESH,
        )

    def t_copy(block, to):
        return pltpu.make_async_remote_copy(
            src_ref=tab.at[block], dst_ref=tab.at[block],
            send_sem=t_send.at[to], recv_sem=t_recv.at[block],
            device_id=(to, fs), device_id_type=MESH,
        )

    def across(step):
        return ((y_at + step) % rows_y) * CORES + core

    w_own(0)
    inputs = hidden[...].astype(F32)
    factor = lax.rsqrt(jnp.mean(inputs * inputs, axis=-1, keepdims=True) + EPSILON)
    normed[pl.ds(aligned(ctx, tok), tok), :] = (inputs * factor * norm_gain[...]).astype(BF)
    for step in range(1, rows_y):
        h_copy(ctx, across(step), h_send.at[step]).start()
    h_copy(ctx, sibling, h_send.at[0]).start()
    for step in range(1, ctx_n):
        t_copy(ctx, (ctx + step) % ctx_n).start()

    def entry(table, column):
        at = (lax.broadcasted_iota(jnp.int32, table.shape, 0) == column) & (
            lax.broadcasted_iota(jnp.int32, table.shape, 1) == fs
        )
        row = jnp.sum(jnp.where(at, table[...].astype(F32), 0.0), axis=0, keepdims=True)
        return jnp.sum(row, axis=1, keepdims=True).astype(jnp.int32)

    ends = []
    running = jnp.zeros((1, 1), jnp.int32)
    for j in range(seg_n):
        running = running + entry(lengths, j)
        ends.append(running)

    def first_place(pos):
        first = jnp.zeros_like(pos)
        for end in ends:
            first = jnp.where(pos >= end, end, first)
        return first

    lane = lax.broadcasted_iota(jnp.int32, (1, HEAD_WIDTH), 1)
    half = HEAD_WIDTH // 2
    frequency = jnp.exp(
        (lane % half).astype(F32) * (-2.0 * math.log(THETA) / HEAD_WIDTH)
    )

    def rope_tables(first, last):
        @pl.loop(first, last)
        def _(c):
            pos = lax.broadcasted_iota(jnp.int32, (tok, HEAD_WIDTH), 0) + entry(pieces, c) * tok
            angles = (pos - first_place(pos)).astype(F32) * frequency
            sine = jnp.sin(angles)
            at = pl.ds(aligned(c, tok), tok)
            cos_t[at, :] = jnp.cos(angles)
            sin_t[at, :] = jnp.where(lane < half, -sine, sine)

    w_step(0, 1)
    w_own(1)
    rope_tables(0, ctx_n // 2)
    w_step(0, 2)
    rope_tables(ctx_n // 2, ctx_n)
    w_step(0, 3)
    w_step(1, 1)
    for step in range(1, ctx_n):
        t_copy((ctx + step) % ctx_n, ctx).wait_recv()

    owners = lax.broadcasted_iota(jnp.int32, (total_n, tok), 0)
    before = jnp.where(
        lax.broadcasted_iota(jnp.int32, (tok, tok), 0)
        < lax.broadcasted_iota(jnp.int32, (tok, tok), 1),
        1.0, 0.0,
    ).astype(BF)
    lane_shift = (fs * per) % HEAD_WIDTH
    places = []
    slots = jnp.zeros((total_n, HEAD_WIDTH), F32)
    for c in range(ctx_n):
        owner_row = tab[c, 0:1, :]
        slot_row = tab[c, 1:2, :] + 1
        mine = jnp.where(owners == owner_row, 1.0, 0.0)
        earlier = jnp.dot(mine.astype(BF), before, preferred_element_type=F32)
        rank = jnp.sum(mine * earlier, axis=0, keepdims=True).astype(jnp.int32)
        places.append(owner_row * per + c * most + rank)
        column = rank + (c * most + lane_shift)
        spread = jnp.where(
            lax.broadcasted_iota(jnp.int32, (HEAD_WIDTH, tok), 0) == column, 1.0, 0.0
        ).astype(BF)
        high = (mine * (slot_row // 32).astype(F32)).astype(BF)
        low = (mine * (slot_row % 32).astype(F32)).astype(BF)
        slots = slots + dot_nt(high, spread) * 32.0 + dot_nt(low, spread)
    place_row = jnp.concatenate(places, axis=1)
    slot2d[...] = slots

    @pl.loop(0, total_n)
    def _(o):
        slot_msg[o] = jnp.broadcast_to(slot2d[pl.ds(o, 1), :], (8, HEAD_WIDTH))

    for step in range(1, rows_y):
        block = across(step)
        h_copy(block, sibling, h_send.at[0]).wait_recv()
        h_copy(block, sibling, f_send.at[block]).start()
    w_step(1, 2)
    w_finish(0)
    h_copy(sibling, sibling, h_send.at[0]).wait_recv()
    for step in range(1, rows_y):
        h_copy(((y_at + step) % rows_y) * CORES + 1 - core, sibling, h_send.at[0]).wait_recv()

    def norm_rope(x, gain, cosine, sine):
        scale = lax.rsqrt(jnp.mean(x * x, axis=-1, keepdims=True) + EPSILON)
        y = x * scale * gain
        return (y * cosine + pltpu.roll(y, half, 1) * sine).astype(BF)

    @pl.loop(0, ctx_n)
    def _(c):
        at = pl.ds(aligned(c, tok), tok)
        raw = jnp.dot(normed[at, :], wkv[...], preferred_element_type=F32)
        cosine, sine = cos_t[at, :], sin_t[at, :]
        for h in range(kc // HEAD_WIDTH):
            cols = slice(h * HEAD_WIDTH, (h + 1) * HEAD_WIDTH)
            kv[at, cols] = norm_rope(raw[:, cols], k_gain[...], cosine, sine)
        kv[at, kc : 2 * kc] = raw[:, kc:].astype(BF)

    def c_copy(to, sender):
        return pltpu.make_async_remote_copy(
            src_ref=bucket.at[pl.ds(aligned(to, per), per), :],
            dst_ref=got.at[sender // fsdp_n, pl.ds(aligned(sender % fsdp_n, per), per), :],
            send_sem=c_send.at[to], recv_sem=c_recv.at[sender],
            device_id=(to // fsdp_n, to % fsdp_n), device_id_type=MESH,
        )

    def s_copy(to, sender):
        return pltpu.make_async_remote_copy(
            src_ref=slot_msg.at[to], dst_ref=slot_got.at[sender],
            send_sem=s_send.at[to], recv_sem=s_recv.at[sender],
            device_id=(to // fsdp_n, to % fsdp_n), device_id_type=MESH,
        )

    w_step(1, 3)
    chunk = 256
    chunks = total_n * per // chunk
    reach = chunk // per

    @pl.loop(0, chunks)
    def _(step):
        i = (me // reach + 1 + 2 * (step % (chunks // 2)) + step // (chunks // 2)) % chunks
        rows = lax.broadcasted_iota(jnp.int32, (chunk, ctx_n * tok), 0) + i * chunk
        pick = jnp.where(rows == place_row, 1.0, 0.0).astype(BF)
        bucket[pl.ds(aligned(i, chunk), chunk), :] = jnp.dot(
            pick, kv[...], preferred_element_type=F32
        ).astype(BF)

        @pl.loop(0, reach)
        def _(inner):
            to = i * reach + (me + inner) % reach

            @pl.when(to != me)
            def _():
                c_copy(to, me).start()

                @pl.when(ctx == 0)
                def _():
                    s_copy(to, fs).start()

    got[ctx, pl.ds(aligned(fs, per), per), :] = bucket[pl.ds(aligned(me, per), per), :]

    @pl.when(ctx == 0)
    def _():
        slot_got[fs] = slot_msg[me]

    w_finish(1)

    @pl.loop(0, ctx_n)
    def _(c):
        at = pl.ds(aligned(c, tok), tok)
        raw = jnp.dot(normed[at, :], wq[...], preferred_element_type=F32)
        cosine, sine = cos_t[at, :], sin_t[at, :]
        for h in range(qc // HEAD_WIDTH):
            cols = slice(h * HEAD_WIDTH, (h + 1) * HEAD_WIDTH)
            q_rows[at, cols] = norm_rope(raw[:, cols], q_gain[...], cosine, sine)

    key_pos = jnp.concatenate(
        [
            lax.broadcasted_iota(jnp.int32, (1, tok), 1) + entry(pieces, c) * tok
            for c in range(ctx_n)
        ],
        axis=1,
    )

    def a_copy(block, sender):
        return pltpu.make_async_remote_copy(
            src_ref=attn.at[pl.ds(aligned(block, tok), tok), :], dst_ref=attn_got.at[sender],
            send_sem=a_send.at[block], recv_sem=a_recv.at[sender],
            device_id=(block, fs), device_id_type=MESH,
        )

    group_width = qc // kc

    @pl.loop(0, ctx_n)
    def _(step):
        c = (ctx + 1 + step) % ctx_n
        at = pl.ds(aligned(c, tok), tok)
        pos = lax.broadcasted_iota(jnp.int32, (tok, 1), 0) + entry(pieces, c) * tok
        visible = (key_pos <= pos) & (key_pos >= first_place(pos))
        for h in range(qc // HEAD_WIDTH):
            j = h // group_width
            cols = slice(h * HEAD_WIDTH, (h + 1) * HEAD_WIDTH)
            keys = kv[:, j * HEAD_WIDTH : (j + 1) * HEAD_WIDTH]
            values = kv[:, kc + j * HEAD_WIDTH : kc + (j + 1) * HEAD_WIDTH]
            scores = dot_nt(q_rows[at, cols], keys)
            masked = jnp.where(visible, scores, NEG_BIG)
            weights = jnp.exp2((masked - jnp.max(masked, axis=-1, keepdims=True)) * EXPONENT)
            total = jnp.sum(weights, axis=-1, keepdims=True)
            mixed = jnp.dot(weights.astype(BF), values, preferred_element_type=F32)
            attn[at, cols] = (mixed / total).astype(BF)

        @pl.when(step < ctx_n - 1)
        def _():
            a_copy(c, ctx).start()

    attn_got[ctx] = attn[pl.ds(aligned(ctx, tok), tok), :]

    for g in range(fsdp_n):
        @pl.when((ctx > 0) | (fs != g))
        def _():
            s_copy(me, g).wait_recv()

    shared = HEAD_WIDTH // per
    slot_line = jnp.concatenate(
        [
            sum(slot_got[p * shared + i, 0:1, :] for i in range(shared))
            for p in range(fsdp_n // shared)
        ],
        axis=1,
    )
    line_out[...] = jnp.broadcast_to(slot_line, line_out.shape)

    def out_copy(which, c):
        source, target = ((attn_got, attn_out), (got, got_out))[which]
        return pltpu.make_async_copy(source.at[c], target.at[c], o_sem.at[which, c])

    out_copy(0, ctx).start()
    for step in range(1, ctx_n):
        sender = (ctx + step) % ctx_n
        a_copy(ctx, sender).wait_recv()
        out_copy(0, sender).start()

    for step in range(ctx_n):
        sender = (ctx + step) % ctx_n

        @pl.loop(1 if step == 0 else 0, fsdp_n)
        def _(g):
            c_copy(me, sender * fsdp_n + (fs + g) % fsdp_n).wait_recv()

        out_copy(1, sender).start()

    w_sent(0)
    w_sent(1)
    for step in range(1, rows_y):
        h_copy(ctx, across(step), h_send.at[step]).wait_send()
        block = across(step)
        h_copy(block, sibling, f_send.at[block]).wait_send()
    h_copy(ctx, sibling, h_send.at[0]).wait_send()
    for step in range(1, ctx_n):
        t_copy(ctx, (ctx + step) % ctx_n).wait_send()
        a_copy((ctx + step) % ctx_n, ctx).wait_send()

    @pl.loop(1, total_n)
    def _(step):
        to = (me + step) % total_n
        c_copy(to, me).wait_send()

        @pl.when(ctx == 0)
        def _():
            s_copy(to, fs).wait_send()

    for c in range(ctx_n):
        out_copy(0, c).wait()
        out_copy(1, c).wait()


def place_rows(
    line, got, heads, cache, attended, rows, placed, place, in_sem, out_sem, head_sem
):
    ctx_n, qc = heads.shape[0], heads.shape[2]
    kc = got.shape[2] // 2

    def rows_in(c):
        return pltpu.make_async_copy(got.at[c], rows.at[c], in_sem.at[c])

    def rows_out(c, half):
        return pltpu.make_async_copy(
            placed.at[c, :, half * kc : (half + 1) * kc],
            cache.at[:, (half * ctx_n + c) * kc : (half * ctx_n + c + 1) * kc],
            out_sem.at[half, c],
        )

    def heads_across(c):
        return pltpu.make_async_copy(
            heads.at[c], attended.at[:, c * qc : (c + 1) * qc], head_sem.at[c]
        )

    for c in range(ctx_n):
        rows_in(c).start()
    for c in range(ctx_n):
        heads_across(c).start()
    spot = lax.broadcasted_iota(jnp.int32, place.shape, 0) + 1
    place[...] = jnp.where(spot == line[0:1, :].astype(jnp.int32), 1.0, 0.0).astype(BF)
    for c in range(ctx_n):
        rows_in(c).wait()
        placed[c] = jnp.dot(place[...], rows[c], preferred_element_type=F32).astype(BF)
        rows_out(c, 0).start()
        rows_out(c, 1).start()
    for c in range(ctx_n):
        heads_across(c).wait()
        rows_out(c, 0).wait()
        rows_out(c, 1).wait()


def shards(
    ctx_n, fsdp_n,
    hidden, norm_gain, w_query, w_key, w_value, q_gain, k_gain, lengths, piece_map, owner, slot,
):
    tok, width = hidden.shape[2:]
    kc, qc = w_key.shape[1], w_query.shape[1]
    total_n = ctx_n * fsdp_n
    most = 2 * tok // total_n
    per = ctx_n * most
    stream = ctx_n * tok
    minor_n = fsdp_n // LINE
    vmem = pl.BlockSpec(memory_space=pltpu.VMEM)
    anywhere = pl.BlockSpec(memory_space=pl.ANY)
    dma = pltpu.SemaphoreType.DMA
    cap = total_n * most
    heads, got, line = pl.pallas_call(
        functools.partial(kernel, ctx_n, fsdp_n, lengths.shape[1]),
        out_shape=(
            jax.ShapeDtypeStruct((ctx_n, tok, qc), BF),
            jax.ShapeDtypeStruct((ctx_n, fsdp_n * per, 2 * kc), BF),
            jax.ShapeDtypeStruct((8, fsdp_n * per), F32),
        ),
        in_specs=[vmem] * 11,
        out_specs=(anywhere, anywhere, vmem),
        scratch_shapes=[
            pltpu.VMEM((stream, width), BF),
            pltpu.VMEM((width, 2 * kc), BF),
            pltpu.VMEM((width, qc), BF),
            pltpu.VMEM((ctx_n, 8, tok), jnp.int32),
            pltpu.VMEM((stream, HEAD_WIDTH), F32),
            pltpu.VMEM((stream, HEAD_WIDTH), F32),
            pltpu.VMEM((stream, 2 * kc), BF),
            pltpu.VMEM((stream, qc), BF),
            pltpu.VMEM((total_n * per, 2 * kc), BF),
            pltpu.VMEM((ctx_n, fsdp_n * per, 2 * kc), BF),
            pltpu.VMEM((total_n, HEAD_WIDTH), F32),
            pltpu.VMEM((total_n, 8, HEAD_WIDTH), F32),
            pltpu.VMEM((fsdp_n, 8, HEAD_WIDTH), F32),
            pltpu.VMEM((stream, qc), BF),
            pltpu.VMEM((ctx_n, tok, qc), BF),
            dma((2, minor_n + 1, fsdp_n)),
            dma((2, fsdp_n)),
            dma((ctx_n,)),
            dma((ctx_n,)),
            dma((ctx_n,)),
            dma((ctx_n,)),
            dma((ctx_n,)),
            dma((total_n,)),
            dma((total_n,)),
            dma((total_n,)),
            dma((fsdp_n,)),
            dma((ctx_n,)),
            dma((ctx_n,)),
            dma((2, ctx_n)),
        ],
        compiler_params=pltpu.CompilerParams(
            collective_id=0, has_side_effects=True, vmem_limit_bytes=56 * 1024 * 1024
        ),
        name="prefill",
    )(
        lengths.T, piece_map.T, hidden[0, 0], norm_gain[None], w_query, w_key, w_value,
        q_gain[None], k_gain[None], owner[0], slot[0],
    )
    cache, attended = pl.pallas_call(
        place_rows,
        out_shape=(
            jax.ShapeDtypeStruct((cap, 2 * ctx_n * kc), BF),
            jax.ShapeDtypeStruct((tok, ctx_n * qc), BF),
        ),
        in_specs=[vmem, anywhere, anywhere],
        out_specs=(anywhere, anywhere),
        scratch_shapes=[
            pltpu.VMEM((ctx_n, fsdp_n * per, 2 * kc), BF),
            pltpu.VMEM((ctx_n, cap, 2 * kc), BF),
            pltpu.VMEM((cap, fsdp_n * per), BF),
            dma((ctx_n,)),
            dma((2, ctx_n)),
            dma((ctx_n,)),
        ],
        compiler_params=pltpu.CompilerParams(vmem_limit_bytes=56 * 1024 * 1024),
        name="place_rows",
    )(line, got, heads)
    return (attended[None, None], cache)


def solution(mesh):
    placed = (
        P("ctx", "fsdp", None, None),
        P(),
        P("fsdp", "ctx"),
        P("fsdp", "ctx"),
        P("fsdp", "ctx"),
        P(),
        P(),
        P(),
        P(),
        P("ctx", "fsdp", None),
        P("ctx", "fsdp", None),
    )
    return jax.shard_map(
        functools.partial(shards, mesh.shape["ctx"], mesh.shape["fsdp"]),
        mesh=mesh,
        in_specs=placed,
        out_specs=(P("ctx", "fsdp", None, None), P(("ctx", "fsdp"), None)),
        check_vma=False,
    )
```

```python
import functools
import math

import jax
import jax.numpy as jnp
from jax import lax
from jax.experimental import pallas as pl
from jax.experimental.pallas import tpu as pltpu
from jax.sharding import PartitionSpec as P

HEAD_WIDTH = 128
EPSILON = 1e-06
THETA = 1000000.0
NEG_BIG = -1e30
EXPONENT = math.log2(math.e) / math.sqrt(HEAD_WIDTH)
MESH = pl.DeviceIdType.MESH
LINE = 4
CORES = 2
BF = jnp.bfloat16
F32 = jnp.float32


def dot_nt(a, b):
    return lax.dot_general(a, b, (((1,), (1,)), ((), ())), preferred_element_type=F32)


def aligned(index, size):
    return pl.multiple_of(index * size, size)


def kernel(
    ctx_n, fsdp_n, seg_n,
    lengths, pieces, hidden, norm_gain, w_q, w_k, w_v, q_gain, k_gain, owner, slot,
    attn_out, got_out, line_out,
    normed, wkv, wq, tab, cos_t, sin_t, kv, q_rows, bucket, got, slot2d, slot_msg, slot_got,
    attn, attn_got,
    w_send, w_recv, h_send, h_recv, f_send, t_send, t_recv,
    c_send, c_recv, s_send, s_recv, a_send, a_recv, o_sem,
):
    ctx = lax.axis_index("ctx")
    fs = lax.axis_index("fsdp")
    me = ctx * fsdp_n + fs
    total_n = ctx_n * fsdp_n
    tok = hidden.shape[0]
    wide = w_q.shape[0]
    kc = w_k.shape[1]
    qc = w_q.shape[1]
    per = got.shape[1] // fsdp_n
    most = per // ctx_n
    minor_n = fsdp_n // LINE
    rows_y = ctx_n // CORES
    phases = bucket.shape[0]
    part = per // phases
    pair = CORES * tok
    major, minor = fs // minor_n, fs % minor_n
    y_at, core = ctx // CORES, ctx % CORES
    sibling = y_at * CORES + (1 - core)

    barrier = pltpu.get_barrier_semaphore()

    @pl.loop(1, total_n)
    def _(step):
        other = (me + step) % total_n
        pl.semaphore_signal(
            barrier, inc=1, device_id=(other // fsdp_n, other % fsdp_n), device_id_type=MESH
        )

    wkv[pl.ds(aligned(fs, wide), wide), 0:kc] = w_k[...]
    wkv[pl.ds(aligned(fs, wide), wide), kc : 2 * kc] = w_v[...]
    wq[pl.ds(aligned(fs, wide), wide), :] = w_q[...]
    tab[ctx] = jnp.concatenate(
        [owner[...], slot[...], jnp.zeros((6, tok), jnp.int32)], axis=0
    )
    pl.semaphore_wait(barrier, total_n - 1)

    buffers = (wkv, wq)

    def w_copy(part, target, shard):
        spot = buffers[part].at[pl.ds(aligned(shard, wide), wide), :]
        to = ((fs + minor_n) % fsdp_n, (fs + fsdp_n - minor_n) % fsdp_n)[target] if target < 2 else (
            major * minor_n + (minor + target - 1) % minor_n
        )
        return pltpu.make_async_remote_copy(
            src_ref=spot, dst_ref=spot,
            send_sem=w_send.at[part, target, shard], recv_sem=w_recv.at[part, shard],
            device_id=(ctx, to), device_id_type=MESH,
        )

    def w_minors(part, shard):
        for target in range(2, minor_n + 1):
            w_copy(part, target, shard).start()

    def w_own(part):
        @pl.when(major < LINE - 1)
        def _():
            w_copy(part, 0, fs).start()

        @pl.when(major > 0)
        def _():
            w_copy(part, 1, fs).start()

        w_minors(part, fs)

    def w_step(part, k):
        @pl.when(major - k >= 0)
        def _():
            shard = fs - k * minor_n
            w_copy(part, 0, shard).wait_recv()

            @pl.when(major < LINE - 1)
            def _():
                w_copy(part, 0, shard).start()

            w_minors(part, shard)

        @pl.when(major + k < LINE)
        def _():
            shard = fs + k * minor_n
            w_copy(part, 1, shard).wait_recv()

            @pl.when(major > 0)
            def _():
                w_copy(part, 1, shard).start()

            w_minors(part, shard)

    def w_finish(part):
        for step in range(1, minor_n):
            for line in range(LINE):
                w_copy(part, 0, line * minor_n + (minor + step) % minor_n).wait_recv()

    def w_sent(part):
        for line in range(LINE):
            shard = line * minor_n + minor

            @pl.when((major < LINE - 1) & (line <= major))
            def _():
                w_copy(part, 0, shard).wait_send()

            @pl.when((major > 0) & (line >= major))
            def _():
                w_copy(part, 1, shard).wait_send()

            for target in range(2, minor_n + 1):
                w_copy(part, target, shard).wait_send()

    def h_copy(block, to, send_sem):
        spot = normed.at[pl.ds(aligned(block, tok), tok), :]
        return pltpu.make_async_remote_copy(
            src_ref=spot, dst_ref=spot, send_sem=send_sem, recv_sem=h_recv.at[block],
            device_id=(to, fs), device_id_type=MESH,
        )

    def t_copy(block, to):
        return pltpu.make_async_remote_copy(
            src_ref=tab.at[block], dst_ref=tab.at[block],
            send_sem=t_send.at[to], recv_sem=t_recv.at[block],
            device_id=(to, fs), device_id_type=MESH,
        )

    def across(step):
        return ((y_at + step) % rows_y) * CORES + core

    w_own(0)
    inputs = hidden[...].astype(F32)
    factor = lax.rsqrt(jnp.mean(inputs * inputs, axis=-1, keepdims=True) + EPSILON)
    normed[pl.ds(aligned(ctx, tok), tok), :] = (inputs * factor * norm_gain[...]).astype(BF)
    for step in range(1, rows_y):
        h_copy(ctx, across(step), h_send.at[step]).start()
    h_copy(ctx, sibling, h_send.at[0]).start()
    for step in range(1, ctx_n):
        t_copy(ctx, (ctx + step) % ctx_n).start()

    def entry(table, column):
        at = (lax.broadcasted_iota(jnp.int32, table.shape, 0) == column) & (
            lax.broadcasted_iota(jnp.int32, table.shape, 1) == fs
        )
        row = jnp.sum(jnp.where(at, table[...].astype(F32), 0.0), axis=0, keepdims=True)
        return jnp.sum(row, axis=1, keepdims=True).astype(jnp.int32)

    ends = []
    running = jnp.zeros((1, 1), jnp.int32)
    for j in range(seg_n):
        running = running + entry(lengths, j)
        ends.append(running)

    def first_place(pos):
        first = jnp.zeros_like(pos)
        for end in ends:
            first = jnp.where(pos >= end, end, first)
        return first

    lane = lax.broadcasted_iota(jnp.int32, (1, HEAD_WIDTH), 1)
    half = HEAD_WIDTH // 2
    frequency = jnp.exp(
        (lane % half).astype(F32) * (-2.0 * math.log(THETA) / HEAD_WIDTH)
    )

    step_angles = lax.broadcasted_iota(jnp.int32, (tok, HEAD_WIDTH), 0).astype(F32) * frequency
    step_cos, step_sin = jnp.cos(step_angles), jnp.sin(step_angles)

    w_step(0, 1)
    w_own(1)

    @pl.loop(0, ctx_n)
    def _(c):
        start = entry(pieces, c) * tok
        pos = lax.broadcasted_iota(jnp.int32, (tok, HEAD_WIDTH), 0) + start
        firsts = [jnp.zeros((1, 1), jnp.int32)] + ends[:-1]
        shift = jnp.concatenate(
            [(start - first).astype(F32) * frequency for first in firsts], axis=0
        )
        shift_cos, shift_sin = jnp.cos(shift), jnp.sin(shift)
        row_cos = jnp.broadcast_to(shift_cos[0:1, :], pos.shape)
        row_sin = jnp.broadcast_to(shift_sin[0:1, :], pos.shape)
        for j in range(1, seg_n):
            later = pos >= firsts[j]
            row_cos = jnp.where(later, shift_cos[j : j + 1, :], row_cos)
            row_sin = jnp.where(later, shift_sin[j : j + 1, :], row_sin)
        at = pl.ds(aligned(c, tok), tok)
        sine = step_sin * row_cos + step_cos * row_sin
        cos_t[at, :] = step_cos * row_cos - step_sin * row_sin
        sin_t[at, :] = jnp.where(lane < half, -sine, sine)

    w_step(0, 2)
    for step in range(1, ctx_n):
        t_copy((ctx + step) % ctx_n, ctx).wait_recv()

    owners = lax.broadcasted_iota(jnp.int32, (total_n, tok), 0)
    before = jnp.where(
        lax.broadcasted_iota(jnp.int32, (tok, tok), 0)
        < lax.broadcasted_iota(jnp.int32, (tok, tok), 1),
        1.0, 0.0,
    ).astype(BF)
    lane_shift = (fs * per) % HEAD_WIDTH
    slots = jnp.zeros((total_n, HEAD_WIDTH), F32)

    def phase_blocks(phase):
        if phases == 1:
            return list(range(ctx_n))
        return [((y_at + phase) % rows_y) * CORES + i for i in range(CORES)]

    places = [[] for _ in range(phases)]
    for phase, spot, c in [
        (phase, spot, c) for phase in range(phases) for spot, c in enumerate(phase_blocks(phase))
    ]:
        owner_row = tab[c, 0:1, :]
        slot_row = tab[c, 1:2, :] + 1
        mine = jnp.where(owners == owner_row, 1.0, 0.0)
        earlier = jnp.dot(mine.astype(BF), before, preferred_element_type=F32)
        rank = jnp.sum(mine * earlier, axis=0, keepdims=True).astype(jnp.int32)
        places[phase].append(owner_row * part + spot * most + rank)
        column = rank + (c * most + lane_shift)
        spread = jnp.where(
            lax.broadcasted_iota(jnp.int32, (HEAD_WIDTH, tok), 0) == column, 1.0, 0.0
        ).astype(BF)
        high = (mine * (slot_row // 32).astype(F32)).astype(BF)
        low = (mine * (slot_row % 32).astype(F32)).astype(BF)
        slots = slots + dot_nt(high, spread) * 32.0 + dot_nt(low, spread)
    place_rows_of = [jnp.concatenate(found, axis=1) for found in places]
    slot2d[...] = slots

    @pl.loop(0, total_n)
    def _(o):
        slot_msg[o] = jnp.broadcast_to(slot2d[pl.ds(o, 1), :], (8, HEAD_WIDTH))

    def norm_rope(x, gain, cosine, sine):
        scale = lax.rsqrt(jnp.mean(x * x, axis=-1, keepdims=True) + EPSILON)
        y = x * scale * gain
        return (y * cosine + pltpu.roll(y, half, 1) * sine).astype(BF)

    def kv_rows(y):
        at = pl.ds(aligned(y, pair), pair)
        raw = jnp.dot(normed[at, :], wkv[...], preferred_element_type=F32)
        cosine, sine = cos_t[at, :], sin_t[at, :]
        for h in range(kc // HEAD_WIDTH):
            cols = slice(h * HEAD_WIDTH, (h + 1) * HEAD_WIDTH)
            kv[at, cols] = norm_rope(raw[:, cols], k_gain[...], cosine, sine)
        kv[at, kc : 2 * kc] = raw[:, kc:].astype(BF)

    def c_copy(to, sender, phase):
        shift = ((sender // (fsdp_n * CORES) + phase) % phases) * part
        begin = pl.multiple_of((sender % fsdp_n) * per + shift, part)
        return pltpu.make_async_remote_copy(
            src_ref=bucket.at[phase, pl.ds(aligned(to, part), part), :],
            dst_ref=got.at[sender // fsdp_n, pl.ds(begin, part), :],
            send_sem=c_send.at[phase, to], recv_sem=c_recv.at[phase, sender],
            device_id=(to // fsdp_n, to % fsdp_n), device_id_type=MESH,
        )

    def s_copy(to, sender):
        return pltpu.make_async_remote_copy(
            src_ref=slot_msg.at[to], dst_ref=slot_got.at[sender],
            send_sem=s_send.at[to], recv_sem=s_recv.at[sender],
            device_id=(to // fsdp_n, to % fsdp_n), device_id_type=MESH,
        )

    chunk = 256
    chunks = total_n * part // chunk
    reach = chunk // part
    near = reach // 2

    def send_phase(phase):
        spread = place_rows_of[phase]
        if phases == 1:
            tokens = pl.ds(0, ctx_n * tok)
        else:
            tokens = pl.ds(aligned((y_at + phase) % rows_y, pair), pair)

        @pl.loop(0, chunks)
        def _(step):
            i = (me // reach + 1 + step) % chunks
            rows = lax.broadcasted_iota(jnp.int32, (chunk, spread.shape[1]), 0) + i * chunk
            pick = jnp.where(rows == spread, 1.0, 0.0).astype(BF)
            bucket[phase, pl.ds(aligned(i, chunk), chunk), :] = jnp.dot(
                pick, kv[tokens, :], preferred_element_type=F32
            ).astype(BF)

            @pl.loop(0, reach)
            def _(inner):
                base = me % reach
                side = (base // near + 1 + inner // near) % 2
                to = i * reach + side * near + (base + inner) % near

                @pl.when(to != me)
                def _():
                    c_copy(to, me, phase).start()

                    if phase == 0:
                        @pl.when(ctx == 0)
                        def _():
                            s_copy(to, fs).start()

        begin = pl.multiple_of(fs * per + ((y_at + phase) % phases) * part, part)
        got[ctx, pl.ds(begin, part), :] = bucket[phase, pl.ds(aligned(me, part), part), :]

    w_step(0, 3)
    w_step(1, 1)
    w_finish(0)
    h_copy(sibling, sibling, h_send.at[0]).wait_recv()
    kv_rows(y_at)
    for step in range(1, rows_y):
        block = across(step)
        h_copy(block, sibling, h_send.at[0]).wait_recv()
        h_copy(block, sibling, f_send.at[block]).start()
    w_step(1, 2)
    if phases == 2:
        send_phase(0)
    for step in range(1, rows_y):
        h_copy(((y_at + step) % rows_y) * CORES + 1 - core, sibling, h_send.at[0]).wait_recv()
        kv_rows((y_at + step) % rows_y)
    w_step(1, 3)
    send_phase(phases - 1)

    @pl.when(ctx == 0)
    def _():
        slot_got[fs] = slot_msg[me]

    w_finish(1)

    @pl.loop(0, rows_y)
    def _(y):
        at = pl.ds(aligned(y, pair), pair)
        raw = jnp.dot(normed[at, :], wq[...], preferred_element_type=F32)
        cosine, sine = cos_t[at, :], sin_t[at, :]
        for h in range(qc // HEAD_WIDTH):
            cols = slice(h * HEAD_WIDTH, (h + 1) * HEAD_WIDTH)
            q_rows[at, cols] = norm_rope(raw[:, cols], q_gain[...], cosine, sine)

    key_pos = jnp.concatenate(
        [
            lax.broadcasted_iota(jnp.int32, (1, tok), 1) + entry(pieces, c) * tok
            for c in range(ctx_n)
        ],
        axis=1,
    )

    def a_copy(block, sender):
        return pltpu.make_async_remote_copy(
            src_ref=attn.at[pl.ds(aligned(block, tok), tok), :], dst_ref=attn_got.at[sender],
            send_sem=a_send.at[block], recv_sem=a_recv.at[sender],
            device_id=(block, fs), device_id_type=MESH,
        )

    group_width = qc // kc

    @pl.loop(0, ctx_n)
    def _(step):
        c = (ctx + 1 + step) % ctx_n
        at = pl.ds(aligned(c, tok), tok)
        pos = lax.broadcasted_iota(jnp.int32, (tok, 1), 0) + entry(pieces, c) * tok
        visible = (key_pos <= pos) & (key_pos >= first_place(pos))
        for h in range(qc // HEAD_WIDTH):
            j = h // group_width
            cols = slice(h * HEAD_WIDTH, (h + 1) * HEAD_WIDTH)
            keys = kv[:, j * HEAD_WIDTH : (j + 1) * HEAD_WIDTH]
            values = kv[:, kc + j * HEAD_WIDTH : kc + (j + 1) * HEAD_WIDTH]
            scores = dot_nt(q_rows[at, cols], keys)
            masked = jnp.where(visible, scores, NEG_BIG)
            weights = jnp.exp2((masked - jnp.max(masked, axis=-1, keepdims=True)) * EXPONENT)
            total = jnp.sum(weights, axis=-1, keepdims=True)
            mixed = jnp.dot(weights.astype(BF), values, preferred_element_type=F32)
            attn[at, cols] = (mixed / total).astype(BF)

        @pl.when(step < ctx_n - 1)
        def _():
            a_copy(c, ctx).start()

    attn_got[ctx] = attn[pl.ds(aligned(ctx, tok), tok), :]

    for g in range(fsdp_n):
        @pl.when((ctx > 0) | (fs != g))
        def _():
            s_copy(me, g).wait_recv()

    shared = HEAD_WIDTH // per
    slot_line = jnp.concatenate(
        [
            sum(slot_got[p * shared + i, 0:1, :] for i in range(shared))
            for p in range(fsdp_n // shared)
        ],
        axis=1,
    )
    line_out[...] = jnp.broadcast_to(slot_line, line_out.shape)

    def out_copy(which, c):
        source, target = ((attn_got, attn_out), (got, got_out))[which]
        return pltpu.make_async_copy(source.at[c], target.at[c], o_sem.at[which, c])

    out_copy(0, ctx).start()
    for step in range(1, ctx_n):
        sender = (ctx + step) % ctx_n
        a_copy(ctx, sender).wait_recv()
        out_copy(0, sender).start()

    for step in range(ctx_n):
        sender = (ctx + step) % ctx_n

        @pl.loop(1 if step == 0 else 0, fsdp_n)
        def _(g):
            for phase in range(phases):
                c_copy(me, sender * fsdp_n + (fs + g) % fsdp_n, phase).wait_recv()

        out_copy(1, sender).start()

    w_sent(0)
    w_sent(1)
    for step in range(1, rows_y):
        h_copy(ctx, across(step), h_send.at[step]).wait_send()
        block = across(step)
        h_copy(block, sibling, f_send.at[block]).wait_send()
    h_copy(ctx, sibling, h_send.at[0]).wait_send()
    for step in range(1, ctx_n):
        t_copy(ctx, (ctx + step) % ctx_n).wait_send()
        a_copy((ctx + step) % ctx_n, ctx).wait_send()

    @pl.loop(1, total_n)
    def _(step):
        to = (me + step) % total_n
        for phase in range(phases):
            c_copy(to, me, phase).wait_send()

        @pl.when(ctx == 0)
        def _():
            s_copy(to, fs).wait_send()

    for c in range(ctx_n):
        out_copy(0, c).wait()
        out_copy(1, c).wait()


def place_rows(
    line, got, heads, cache, attended, rows, placed, held, place, in_sem, out_sem, held_sem, head_sem
):
    ctx_n, qc = heads.shape[0], heads.shape[2]
    kc = got.shape[2] // 2

    def rows_in(c):
        return pltpu.make_async_copy(got.at[c], rows.at[c], in_sem.at[c])

    def rows_out(c, half):
        return pltpu.make_async_copy(
            placed.at[c, :, half * kc : (half + 1) * kc],
            cache.at[:, (half * ctx_n + c) * kc : (half * ctx_n + c + 1) * kc],
            out_sem.at[half, c],
        )

    def heads_in(c):
        return pltpu.make_async_copy(heads.at[c], held.at[c], held_sem.at[c])

    def heads_out(c):
        return pltpu.make_async_copy(
            held.at[c], attended.at[:, c * qc : (c + 1) * qc], head_sem.at[c]
        )

    for c in range(ctx_n):
        rows_in(c).start()
    for c in range(ctx_n):
        heads_in(c).start()
    spot = lax.broadcasted_iota(jnp.int32, place.shape, 0) + 1
    place[...] = jnp.where(spot == line[0:1, :].astype(jnp.int32), 1.0, 0.0).astype(BF)
    for c in range(ctx_n):
        rows_in(c).wait()
        placed[c] = jnp.dot(place[...], rows[c], preferred_element_type=F32).astype(BF)
        rows_out(c, 0).start()
        rows_out(c, 1).start()
        heads_in(c).wait()
        heads_out(c).start()
    for c in range(ctx_n):
        heads_out(c).wait()
        rows_out(c, 0).wait()
        rows_out(c, 1).wait()


def shards(
    ctx_n, fsdp_n,
    hidden, norm_gain, w_query, w_key, w_value, q_gain, k_gain, lengths, piece_map, owner, slot,
):
    tok, width = hidden.shape[2:]
    kc, qc = w_key.shape[1], w_query.shape[1]
    total_n = ctx_n * fsdp_n
    most = 2 * tok // total_n
    per = ctx_n * most
    stream = ctx_n * tok
    minor_n = fsdp_n // LINE
    phases = 2 if ctx_n == 2 * CORES and per // 2 % 16 == 0 else 1
    vmem = pl.BlockSpec(memory_space=pltpu.VMEM)
    anywhere = pl.BlockSpec(memory_space=pl.ANY)
    dma = pltpu.SemaphoreType.DMA
    cap = total_n * most
    heads, got, line = pl.pallas_call(
        functools.partial(kernel, ctx_n, fsdp_n, lengths.shape[1]),
        out_shape=(
            jax.ShapeDtypeStruct((ctx_n, tok, qc), BF),
            jax.ShapeDtypeStruct((ctx_n, fsdp_n * per, 2 * kc), BF),
            jax.ShapeDtypeStruct((8, fsdp_n * per), F32),
        ),
        in_specs=[vmem] * 11,
        out_specs=(anywhere, anywhere, vmem),
        scratch_shapes=[
            pltpu.VMEM((stream, width), BF),
            pltpu.VMEM((width, 2 * kc), BF),
            pltpu.VMEM((width, qc), BF),
            pltpu.VMEM((ctx_n, 8, tok), jnp.int32),
            pltpu.VMEM((stream, HEAD_WIDTH), F32),
            pltpu.VMEM((stream, HEAD_WIDTH), F32),
            pltpu.VMEM((stream, 2 * kc), BF),
            pltpu.VMEM((stream, qc), BF),
            pltpu.VMEM((phases, total_n * per // phases, 2 * kc), BF),
            pltpu.VMEM((ctx_n, fsdp_n * per, 2 * kc), BF),
            pltpu.VMEM((total_n, HEAD_WIDTH), F32),
            pltpu.VMEM((total_n, 8, HEAD_WIDTH), F32),
            pltpu.VMEM((fsdp_n, 8, HEAD_WIDTH), F32),
            pltpu.VMEM((stream, qc), BF),
            pltpu.VMEM((ctx_n, tok, qc), BF),
            dma((2, minor_n + 1, fsdp_n)),
            dma((2, fsdp_n)),
            dma((ctx_n,)),
            dma((ctx_n,)),
            dma((ctx_n,)),
            dma((ctx_n,)),
            dma((ctx_n,)),
            dma((phases, total_n)),
            dma((phases, total_n)),
            dma((total_n,)),
            dma((fsdp_n,)),
            dma((ctx_n,)),
            dma((ctx_n,)),
            dma((2, ctx_n)),
        ],
        compiler_params=pltpu.CompilerParams(
            collective_id=0, has_side_effects=True, vmem_limit_bytes=56 * 1024 * 1024
        ),
        name="prefill",
    )(
        lengths.T, piece_map.T, hidden[0, 0], norm_gain[None], w_query, w_key, w_value,
        q_gain[None], k_gain[None], owner[0], slot[0],
    )
    cache, attended = pl.pallas_call(
        place_rows,
        out_shape=(
            jax.ShapeDtypeStruct((cap, 2 * ctx_n * kc), BF),
            jax.ShapeDtypeStruct((tok, ctx_n * qc), BF),
        ),
        in_specs=[vmem, anywhere, anywhere],
        out_specs=(anywhere, anywhere),
        scratch_shapes=[
            pltpu.VMEM((ctx_n, fsdp_n * per, 2 * kc), BF),
            pltpu.VMEM((ctx_n, cap, 2 * kc), BF),
            pltpu.VMEM((ctx_n, tok, qc), BF),
            pltpu.VMEM((cap, fsdp_n * per), BF),
            dma((ctx_n,)),
            dma((2, ctx_n)),
            dma((ctx_n,)),
            dma((ctx_n,)),
        ],
        compiler_params=pltpu.CompilerParams(vmem_limit_bytes=56 * 1024 * 1024),
        name="place_rows",
    )(line, got, heads)
    return (attended[None, None], cache)


def solution(mesh):
    placed = (
        P("ctx", "fsdp", None, None),
        P(),
        P("fsdp", "ctx"),
        P("fsdp", "ctx"),
        P("fsdp", "ctx"),
        P(),
        P(),
        P(),
        P(),
        P("ctx", "fsdp", None),
        P("ctx", "fsdp", None),
    )
    return jax.shard_map(
        functools.partial(shards, mesh.shape["ctx"], mesh.shape["fsdp"]),
        mesh=mesh,
        in_specs=placed,
        out_specs=(P("ctx", "fsdp", None, None), P(("ctx", "fsdp"), None)),
        check_vma=False,
    )
```

```python
import functools
import math

import jax
import jax.numpy as jnp
from jax import lax
from jax.experimental import pallas as pl
from jax.experimental.pallas import tpu as pltpu
from jax.sharding import PartitionSpec as P

HEAD_WIDTH = 128
EPSILON = 1e-06
THETA = 1000000.0
NEG_BIG = -1e30
EXPONENT = math.log2(math.e) / math.sqrt(HEAD_WIDTH)
MESH = pl.DeviceIdType.MESH
LINE = 4
CORES = 2
BF = jnp.bfloat16
F32 = jnp.float32


def dot_nt(a, b):
    return lax.dot_general(a, b, (((1,), (1,)), ((), ())), preferred_element_type=F32)


def aligned(index, size):
    return pl.multiple_of(index * size, size)


def kernel(
    ctx_n, fsdp_n, seg_n,
    lengths, pieces, hidden, norm_gain, w_q, w_k, w_v, q_gain, k_gain, owner, slot,
    attn_out, got_out, line_out,
    normed, wkv, wq, tab, cos_t, sin_t, kv, q_rows, bucket, got, slot2d, slot_msg, slot_got,
    attn, attn_got,
    w_send, w_recv, h_send, h_recv, f_send, t_send, t_recv,
    c_send, c_recv, s_send, s_recv, a_send, a_recv, o_sem,
):
    ctx = lax.axis_index("ctx")
    fs = lax.axis_index("fsdp")
    me = ctx * fsdp_n + fs
    total_n = ctx_n * fsdp_n
    tok = hidden.shape[0]
    wide = w_q.shape[0]
    kc = w_k.shape[1]
    qc = w_q.shape[1]
    per = got.shape[1] // fsdp_n
    most = per // ctx_n
    minor_n = fsdp_n // LINE
    rows_y = ctx_n // CORES
    pair = CORES * tok
    major, minor = fs // minor_n, fs % minor_n
    y_at, core = ctx // CORES, ctx % CORES
    sibling = y_at * CORES + (1 - core)

    barrier = pltpu.get_barrier_semaphore()

    @pl.loop(1, total_n)
    def _(step):
        other = (me + step) % total_n
        pl.semaphore_signal(
            barrier, inc=1, device_id=(other // fsdp_n, other % fsdp_n), device_id_type=MESH
        )

    wkv[pl.ds(aligned(fs, wide), wide), 0:kc] = w_k[...]
    wkv[pl.ds(aligned(fs, wide), wide), kc : 2 * kc] = w_v[...]
    wq[pl.ds(aligned(fs, wide), wide), :] = w_q[...]
    tab[ctx] = jnp.concatenate(
        [owner[...], slot[...], jnp.zeros((6, tok), jnp.int32)], axis=0
    )
    pl.semaphore_wait(barrier, total_n - 1)

    buffers = (wkv, wq)

    def w_copy(part, target, shard):
        spot = buffers[part].at[pl.ds(aligned(shard, wide), wide), :]
        to = ((fs + minor_n) % fsdp_n, (fs + fsdp_n - minor_n) % fsdp_n)[target] if target < 2 else (
            major * minor_n + (minor + target - 1) % minor_n
        )
        return pltpu.make_async_remote_copy(
            src_ref=spot, dst_ref=spot,
            send_sem=w_send.at[part, target, shard], recv_sem=w_recv.at[part, shard],
            device_id=(ctx, to), device_id_type=MESH,
        )

    def w_minors(part, shard):
        for target in range(2, minor_n + 1):
            w_copy(part, target, shard).start()

    def w_own(part):
        @pl.when(major < LINE - 1)
        def _():
            w_copy(part, 0, fs).start()

        @pl.when(major > 0)
        def _():
            w_copy(part, 1, fs).start()

        w_minors(part, fs)

    def w_step(part, k):
        @pl.when(major - k >= 0)
        def _():
            shard = fs - k * minor_n
            w_copy(part, 0, shard).wait_recv()

            @pl.when(major < LINE - 1)
            def _():
                w_copy(part, 0, shard).start()

            w_minors(part, shard)

        @pl.when(major + k < LINE)
        def _():
            shard = fs + k * minor_n
            w_copy(part, 1, shard).wait_recv()

            @pl.when(major > 0)
            def _():
                w_copy(part, 1, shard).start()

            w_minors(part, shard)

    def w_finish(part):
        for step in range(1, minor_n):
            for line in range(LINE):
                w_copy(part, 0, line * minor_n + (minor + step) % minor_n).wait_recv()

    def w_sent(part):
        for line in range(LINE):
            shard = line * minor_n + minor

            @pl.when((major < LINE - 1) & (line <= major))
            def _():
                w_copy(part, 0, shard).wait_send()

            @pl.when((major > 0) & (line >= major))
            def _():
                w_copy(part, 1, shard).wait_send()

            for target in range(2, minor_n + 1):
                w_copy(part, target, shard).wait_send()

    def h_copy(block, to, send_sem):
        spot = normed.at[pl.ds(aligned(block, tok), tok), :]
        return pltpu.make_async_remote_copy(
            src_ref=spot, dst_ref=spot, send_sem=send_sem, recv_sem=h_recv.at[block],
            device_id=(to, fs), device_id_type=MESH,
        )

    def t_copy(block, to):
        return pltpu.make_async_remote_copy(
            src_ref=tab.at[block], dst_ref=tab.at[block],
            send_sem=t_send.at[to], recv_sem=t_recv.at[block],
            device_id=(to, fs), device_id_type=MESH,
        )

    def across(step):
        return ((y_at + step) % rows_y) * CORES + core

    w_own(0)
    inputs = hidden[...].astype(F32)
    factor = lax.rsqrt(jnp.mean(inputs * inputs, axis=-1, keepdims=True) + EPSILON)
    normed[pl.ds(aligned(ctx, tok), tok), :] = (inputs * factor * norm_gain[...]).astype(BF)
    for step in range(1, rows_y):
        h_copy(ctx, across(step), h_send.at[step]).start()
    h_copy(ctx, sibling, h_send.at[0]).start()
    for step in range(1, ctx_n):
        t_copy(ctx, (ctx + step) % ctx_n).start()

    def entry(table, column):
        at = (lax.broadcasted_iota(jnp.int32, table.shape, 0) == column) & (
            lax.broadcasted_iota(jnp.int32, table.shape, 1) == fs
        )
        row = jnp.sum(jnp.where(at, table[...].astype(F32), 0.0), axis=0, keepdims=True)
        return jnp.sum(row, axis=1, keepdims=True).astype(jnp.int32)

    ends = []
    running = jnp.zeros((1, 1), jnp.int32)
    for j in range(seg_n):
        running = running + entry(lengths, j)
        ends.append(running)

    def first_place(pos):
        first = jnp.zeros_like(pos)
        for end in ends:
            first = jnp.where(pos >= end, end, first)
        return first

    lane = lax.broadcasted_iota(jnp.int32, (1, HEAD_WIDTH), 1)
    half = HEAD_WIDTH // 2
    frequency = jnp.exp(
        (lane % half).astype(F32) * (-2.0 * math.log(THETA) / HEAD_WIDTH)
    )

    step_angles = lax.broadcasted_iota(jnp.int32, (tok, HEAD_WIDTH), 0).astype(F32) * frequency
    step_cos, step_sin = jnp.cos(step_angles), jnp.sin(step_angles)

    w_step(0, 1)
    w_own(1)

    @pl.loop(0, ctx_n)
    def _(c):
        start = entry(pieces, c) * tok
        pos = lax.broadcasted_iota(jnp.int32, (tok, HEAD_WIDTH), 0) + start
        firsts = [jnp.zeros((1, 1), jnp.int32)] + ends[:-1]
        shift = jnp.concatenate(
            [(start - first).astype(F32) * frequency for first in firsts], axis=0
        )
        shift_cos, shift_sin = jnp.cos(shift), jnp.sin(shift)
        row_cos = jnp.broadcast_to(shift_cos[0:1, :], pos.shape)
        row_sin = jnp.broadcast_to(shift_sin[0:1, :], pos.shape)
        for j in range(1, seg_n):
            later = pos >= firsts[j]
            row_cos = jnp.where(later, shift_cos[j : j + 1, :], row_cos)
            row_sin = jnp.where(later, shift_sin[j : j + 1, :], row_sin)
        at = pl.ds(aligned(c, tok), tok)
        sine = step_sin * row_cos + step_cos * row_sin
        cos_t[at, :] = step_cos * row_cos - step_sin * row_sin
        sin_t[at, :] = jnp.where(lane < half, -sine, sine)

    w_step(0, 2)
    for step in range(1, ctx_n):
        t_copy((ctx + step) % ctx_n, ctx).wait_recv()

    owners = lax.broadcasted_iota(jnp.int32, (total_n, tok), 0)
    before = jnp.where(
        lax.broadcasted_iota(jnp.int32, (tok, tok), 0)
        < lax.broadcasted_iota(jnp.int32, (tok, tok), 1),
        1.0, 0.0,
    ).astype(BF)
    lane_shift = (fs * per) % HEAD_WIDTH
    slots = jnp.zeros((total_n, HEAD_WIDTH), F32)

    places = []
    for c in range(ctx_n):
        owner_row = tab[c, 0:1, :]
        slot_row = tab[c, 1:2, :] + 1
        mine = jnp.where(owners == owner_row, 1.0, 0.0)
        earlier = jnp.dot(mine.astype(BF), before, preferred_element_type=F32)
        rank = jnp.sum(mine * earlier, axis=0, keepdims=True).astype(jnp.int32)
        places.append(owner_row * per + c * most + rank)
        column = rank + (c * most + lane_shift)
        spread = jnp.where(
            lax.broadcasted_iota(jnp.int32, (HEAD_WIDTH, tok), 0) == column, 1.0, 0.0
        ).astype(BF)
        high = (mine * (slot_row // 32).astype(F32)).astype(BF)
        low = (mine * (slot_row % 32).astype(F32)).astype(BF)
        slots = slots + dot_nt(high, spread) * 32.0 + dot_nt(low, spread)
    place_row = jnp.concatenate(places, axis=1)
    slot2d[...] = slots

    @pl.loop(0, total_n)
    def _(o):
        slot_msg[o] = jnp.broadcast_to(slot2d[pl.ds(o, 1), :], (8, HEAD_WIDTH))

    def norm_rope(x, gain, cosine, sine):
        scale = lax.rsqrt(jnp.mean(x * x, axis=-1, keepdims=True) + EPSILON)
        y = x * scale * gain
        return (y * cosine + pltpu.roll(y, half, 1) * sine).astype(BF)

    def kv_rows(y):
        at = pl.ds(aligned(y, pair), pair)
        raw = jnp.dot(normed[at, :], wkv[...], preferred_element_type=F32)
        cosine, sine = cos_t[at, :], sin_t[at, :]
        for h in range(kc // HEAD_WIDTH):
            cols = slice(h * HEAD_WIDTH, (h + 1) * HEAD_WIDTH)
            kv[at, cols] = norm_rope(raw[:, cols], k_gain[...], cosine, sine)
        kv[at, kc : 2 * kc] = raw[:, kc:].astype(BF)

    def c_copy(to, sender):
        return pltpu.make_async_remote_copy(
            src_ref=bucket.at[pl.ds(aligned(to, per), per), :],
            dst_ref=got.at[sender // fsdp_n, pl.ds(aligned(sender % fsdp_n, per), per), :],
            send_sem=c_send.at[to], recv_sem=c_recv.at[sender],
            device_id=(to // fsdp_n, to % fsdp_n), device_id_type=MESH,
        )

    def s_copy(to, sender):
        return pltpu.make_async_remote_copy(
            src_ref=slot_msg.at[to], dst_ref=slot_got.at[sender],
            send_sem=s_send.at[to], recv_sem=s_recv.at[sender],
            device_id=(to // fsdp_n, to % fsdp_n), device_id_type=MESH,
        )

    w_step(0, 3)
    w_step(1, 1)
    for step in range(1, rows_y):
        block = across(step)
        h_copy(block, sibling, h_send.at[0]).wait_recv()
        h_copy(block, sibling, f_send.at[block]).start()
    w_step(1, 2)
    w_finish(0)
    h_copy(sibling, sibling, h_send.at[0]).wait_recv()
    kv_rows(y_at)
    for step in range(1, rows_y):
        h_copy(((y_at + step) % rows_y) * CORES + 1 - core, sibling, h_send.at[0]).wait_recv()
        kv_rows((y_at + step) % rows_y)
    w_step(1, 3)

    chunk = 256
    chunks = total_n * per // chunk
    reach = chunk // per

    @pl.loop(0, chunks)
    def _(step):
        i = (me // reach + 1 + 2 * (step % (chunks // 2)) + step // (chunks // 2)) % chunks
        rows = lax.broadcasted_iota(jnp.int32, (chunk, ctx_n * tok), 0) + i * chunk
        pick = jnp.where(rows == place_row, 1.0, 0.0).astype(BF)
        bucket[pl.ds(aligned(i, chunk), chunk), :] = jnp.dot(
            pick, kv[...], preferred_element_type=F32
        ).astype(BF)

        @pl.loop(0, reach)
        def _(inner):
            to = i * reach + (me + inner) % reach

            @pl.when(to != me)
            def _():
                c_copy(to, me).start()

                @pl.when(ctx == 0)
                def _():
                    s_copy(to, fs).start()

    got[ctx, pl.ds(aligned(fs, per), per), :] = bucket[pl.ds(aligned(me, per), per), :]

    @pl.when(ctx == 0)
    def _():
        slot_got[fs] = slot_msg[me]

    w_finish(1)

    @pl.loop(0, rows_y)
    def _(y):
        at = pl.ds(aligned(y, pair), pair)
        raw = jnp.dot(normed[at, :], wq[...], preferred_element_type=F32)
        cosine, sine = cos_t[at, :], sin_t[at, :]
        for h in range(qc // HEAD_WIDTH):
            cols = slice(h * HEAD_WIDTH, (h + 1) * HEAD_WIDTH)
            q_rows[at, cols] = norm_rope(raw[:, cols], q_gain[...], cosine, sine)

    key_pos = jnp.concatenate(
        [
            lax.broadcasted_iota(jnp.int32, (1, tok), 1) + entry(pieces, c) * tok
            for c in range(ctx_n)
        ],
        axis=1,
    )

    def a_copy(block, sender):
        return pltpu.make_async_remote_copy(
            src_ref=attn.at[pl.ds(aligned(block, tok), tok), :], dst_ref=attn_got.at[sender],
            send_sem=a_send.at[block], recv_sem=a_recv.at[sender],
            device_id=(block, fs), device_id_type=MESH,
        )

    group_width = qc // kc

    @pl.loop(0, ctx_n)
    def _(step):
        c = (ctx + 1 + step) % ctx_n
        at = pl.ds(aligned(c, tok), tok)
        pos = lax.broadcasted_iota(jnp.int32, (tok, 1), 0) + entry(pieces, c) * tok
        visible = (key_pos <= pos) & (key_pos >= first_place(pos))
        for h in range(qc // HEAD_WIDTH):
            j = h // group_width
            cols = slice(h * HEAD_WIDTH, (h + 1) * HEAD_WIDTH)
            keys = kv[:, j * HEAD_WIDTH : (j + 1) * HEAD_WIDTH]
            values = kv[:, kc + j * HEAD_WIDTH : kc + (j + 1) * HEAD_WIDTH]
            scores = dot_nt(q_rows[at, cols], keys)
            masked = jnp.where(visible, scores, NEG_BIG)
            weights = jnp.exp2((masked - jnp.max(masked, axis=-1, keepdims=True)) * EXPONENT)
            total = jnp.sum(weights, axis=-1, keepdims=True)
            mixed = jnp.dot(weights.astype(BF), values, preferred_element_type=F32)
            attn[at, cols] = (mixed / total).astype(BF)

        @pl.when(step < ctx_n - 1)
        def _():
            a_copy(c, ctx).start()

    attn_got[ctx] = attn[pl.ds(aligned(ctx, tok), tok), :]

    for g in range(fsdp_n):
        @pl.when((ctx > 0) | (fs != g))
        def _():
            s_copy(me, g).wait_recv()

    shared = HEAD_WIDTH // per
    slot_line = jnp.concatenate(
        [
            sum(slot_got[p * shared + i, 0:1, :] for i in range(shared))
            for p in range(fsdp_n // shared)
        ],
        axis=1,
    )
    line_out[...] = jnp.broadcast_to(slot_line, line_out.shape)

    def out_copy(which, c):
        source, target = ((attn_got, attn_out), (got, got_out))[which]
        return pltpu.make_async_copy(source.at[c], target.at[c], o_sem.at[which, c])

    out_copy(0, ctx).start()
    for step in range(1, ctx_n):
        sender = (ctx + step) % ctx_n
        a_copy(ctx, sender).wait_recv()
        out_copy(0, sender).start()

    for step in range(ctx_n):
        sender = (ctx + step) % ctx_n

        @pl.loop(1 if step == 0 else 0, fsdp_n)
        def _(g):
            c_copy(me, sender * fsdp_n + (fs + g) % fsdp_n).wait_recv()

        out_copy(1, sender).start()

    w_sent(0)
    w_sent(1)
    for step in range(1, rows_y):
        h_copy(ctx, across(step), h_send.at[step]).wait_send()
        block = across(step)
        h_copy(block, sibling, f_send.at[block]).wait_send()
    h_copy(ctx, sibling, h_send.at[0]).wait_send()
    for step in range(1, ctx_n):
        t_copy(ctx, (ctx + step) % ctx_n).wait_send()
        a_copy((ctx + step) % ctx_n, ctx).wait_send()

    @pl.loop(1, total_n)
    def _(step):
        to = (me + step) % total_n
        c_copy(to, me).wait_send()

        @pl.when(ctx == 0)
        def _():
            s_copy(to, fs).wait_send()

    for c in range(ctx_n):
        out_copy(0, c).wait()
        out_copy(1, c).wait()


def place_rows(
    line, got, heads, cache, attended, rows, placed, held, place, in_sem, out_sem, held_sem, head_sem
):
    ctx_n, qc = heads.shape[0], heads.shape[2]
    kc = got.shape[2] // 2

    def rows_in(c):
        return pltpu.make_async_copy(got.at[c], rows.at[c], in_sem.at[c])

    def rows_out(c, half):
        return pltpu.make_async_copy(
            placed.at[c, :, half * kc : (half + 1) * kc],
            cache.at[:, (half * ctx_n + c) * kc : (half * ctx_n + c + 1) * kc],
            out_sem.at[half, c],
        )

    def heads_in(c):
        return pltpu.make_async_copy(heads.at[c], held.at[c], held_sem.at[c])

    def heads_out(c):
        return pltpu.make_async_copy(
            held.at[c], attended.at[:, c * qc : (c + 1) * qc], head_sem.at[c]
        )

    for c in range(ctx_n):
        rows_in(c).start()
    for c in range(ctx_n):
        heads_in(c).start()
    spot = lax.broadcasted_iota(jnp.int32, place.shape, 0) + 1
    place[...] = jnp.where(spot == line[0:1, :].astype(jnp.int32), 1.0, 0.0).astype(BF)
    for c in range(ctx_n):
        rows_in(c).wait()
        placed[c] = jnp.dot(place[...], rows[c], preferred_element_type=F32).astype(BF)
        rows_out(c, 0).start()
        rows_out(c, 1).start()
        heads_in(c).wait()
        heads_out(c).start()
    for c in range(ctx_n):
        heads_out(c).wait()
        rows_out(c, 0).wait()
        rows_out(c, 1).wait()


def shards(
    ctx_n, fsdp_n,
    hidden, norm_gain, w_query, w_key, w_value, q_gain, k_gain, lengths, piece_map, owner, slot,
):
    tok, width = hidden.shape[2:]
    kc, qc = w_key.shape[1], w_query.shape[1]
    total_n = ctx_n * fsdp_n
    most = 2 * tok // total_n
    per = ctx_n * most
    stream = ctx_n * tok
    minor_n = fsdp_n // LINE
    vmem = pl.BlockSpec(memory_space=pltpu.VMEM)
    anywhere = pl.BlockSpec(memory_space=pl.ANY)
    dma = pltpu.SemaphoreType.DMA
    cap = total_n * most
    heads, got, line = pl.pallas_call(
        functools.partial(kernel, ctx_n, fsdp_n, lengths.shape[1]),
        out_shape=(
            jax.ShapeDtypeStruct((ctx_n, tok, qc), BF),
            jax.ShapeDtypeStruct((ctx_n, fsdp_n * per, 2 * kc), BF),
            jax.ShapeDtypeStruct((8, fsdp_n * per), F32),
        ),
        in_specs=[vmem] * 11,
        out_specs=(anywhere, anywhere, vmem),
        scratch_shapes=[
            pltpu.VMEM((stream, width), BF),
            pltpu.VMEM((width, 2 * kc), BF),
            pltpu.VMEM((width, qc), BF),
            pltpu.VMEM((ctx_n, 8, tok), jnp.int32),
            pltpu.VMEM((stream, HEAD_WIDTH), F32),
            pltpu.VMEM((stream, HEAD_WIDTH), F32),
            pltpu.VMEM((stream, 2 * kc), BF),
            pltpu.VMEM((stream, qc), BF),
            pltpu.VMEM((total_n * per, 2 * kc), BF),
            pltpu.VMEM((ctx_n, fsdp_n * per, 2 * kc), BF),
            pltpu.VMEM((total_n, HEAD_WIDTH), F32),
            pltpu.VMEM((total_n, 8, HEAD_WIDTH), F32),
            pltpu.VMEM((fsdp_n, 8, HEAD_WIDTH), F32),
            pltpu.VMEM((stream, qc), BF),
            pltpu.VMEM((ctx_n, tok, qc), BF),
            dma((2, minor_n + 1, fsdp_n)),
            dma((2, fsdp_n)),
            dma((ctx_n,)),
            dma((ctx_n,)),
            dma((ctx_n,)),
            dma((ctx_n,)),
            dma((ctx_n,)),
            dma((total_n,)),
            dma((total_n,)),
            dma((total_n,)),
            dma((fsdp_n,)),
            dma((ctx_n,)),
            dma((ctx_n,)),
            dma((2, ctx_n)),
        ],
        compiler_params=pltpu.CompilerParams(
            collective_id=0, has_side_effects=True, vmem_limit_bytes=56 * 1024 * 1024
        ),
        name="prefill",
    )(
        lengths.T, piece_map.T, hidden[0, 0], norm_gain[None], w_query, w_key, w_value,
        q_gain[None], k_gain[None], owner[0], slot[0],
    )
    cache, attended = pl.pallas_call(
        place_rows,
        out_shape=(
            jax.ShapeDtypeStruct((cap, 2 * ctx_n * kc), BF),
            jax.ShapeDtypeStruct((tok, ctx_n * qc), BF),
        ),
        in_specs=[vmem, anywhere, anywhere],
        out_specs=(anywhere, anywhere),
        scratch_shapes=[
            pltpu.VMEM((ctx_n, fsdp_n * per, 2 * kc), BF),
            pltpu.VMEM((ctx_n, cap, 2 * kc), BF),
            pltpu.VMEM((ctx_n, tok, qc), BF),
            pltpu.VMEM((cap, fsdp_n * per), BF),
            dma((ctx_n,)),
            dma((2, ctx_n)),
            dma((ctx_n,)),
            dma((ctx_n,)),
        ],
        compiler_params=pltpu.CompilerParams(vmem_limit_bytes=56 * 1024 * 1024),
        name="place_rows",
    )(line, got, heads)
    return (attended[None, None], cache)


def solution(mesh):
    placed = (
        P("ctx", "fsdp", None, None),
        P(),
        P("fsdp", "ctx"),
        P("fsdp", "ctx"),
        P("fsdp", "ctx"),
        P(),
        P(),
        P(),
        P(),
        P("ctx", "fsdp", None),
        P("ctx", "fsdp", None),
    )
    return jax.shard_map(
        functools.partial(shards, mesh.shape["ctx"], mesh.shape["fsdp"]),
        mesh=mesh,
        in_specs=placed,
        out_specs=(P("ctx", "fsdp", None, None), P(("ctx", "fsdp"), None)),
        check_vma=False,
    )
```
